32 devices in a mesh: smp: 16 (over z, x, core), par: 2 (over y).
Axes of the slice: x: 2, y: 2, z: 4, core: 2. Of those that a mesh axis runs over, the one named last changes fastest.
Arguments:
- log_derivs: float32 [4096, 2048], P('smp', 'par'), may hold values from -40 to 40, as said below
- coefficients: float32 [4096], P('smp'), may hold values from -6 to 6
Outputs:
- gram: float32 [4096, 4096], P('smp', 'par')
- update: float32 [2048], P(('par', 'smp'))
The draws below stay inside these ranges and needn't reach their ends.
Inputs may be any that keep to these rules, and one draw needn't show every extreme that they name: `log_derivs`: finite real values.
All inputs are finite; a program needn't handle non-finite values.
Results may differ from the reference program's by a relative error of at most 0.00014.
Values sent between devices are 32-bit elements; how exact they have to be, the bound alone decides.
No kernel may reach another device: no remote copies, remote signals or barrier semaphores. Data moves between devices by JAX's collectives and lax.ppermute only.
A program may use at most 128 MiB of HBM per device.

```python
import jax
import jax.numpy as jnp
from jax import lax

SAMPLES = 4096
PARAMS = 2048


def draw_log_derivs(key, part):
    keys_split = jax.random.split(jax.random.fold_in(key, 17), 4)
    column_offset = jax.random.uniform(keys_split[0], (PARAMS,), jnp.float32, -1.5, 1.5)
    sample_ramp = 1.0 + 2.0 * jnp.arange(SAMPLES, dtype=jnp.float32) / SAMPLES
    row_scale = jnp.exp(jax.random.uniform(keys_split[1], (SAMPLES, 1), jnp.float32, 0.0, 1.0986))
    column_scale = jnp.exp(jax.random.uniform(keys_split[2], (1, PARAMS), jnp.float32, 0.0, 1.0986))
    noise = jnp.clip(jax.random.normal(keys_split[3], (SAMPLES, PARAMS), jnp.float32), -4.0, 4.0)
    values = column_offset[None, :] * sample_ramp[:, None] + 0.8 * row_scale * column_scale * noise
    return values.astype(jnp.float32)


def steps_of(key, shape, cuts, smallest, top_value):
    factor_of, own = 1.0, jax.random.fold_in(key, 6)
    for axis_at, blocks in cuts:
        draws = jnp.exp(jax.random.uniform(jax.random.fold_in(own, axis_at), (blocks,), jnp.float32, smallest / len(cuts), top_value / len(cuts)))
        factor_of = factor_of * jnp.repeat(draws, shape[axis_at] // blocks).reshape([-1 if axis == axis_at else 1 for axis in range(len(shape))])
    return factor_of


def normal_values(rng, shape, width, limit, shards=(), kind=jnp.bfloat16):
    values = jax.random.normal(rng, shape, jnp.float32) * width
    if len(shards) > 0:
        values = steps_of(rng, shape, shards, -0.22, 0.18) * values
    return jnp.clip(values, min=-limit, max=limit).astype(kind)


def setup_inputs(seed: int = 0) -> dict:
    key_of = jax.random.split(jax.random.key(seed), 3)
    return {
        "log_derivs": draw_log_derivs(jax.random.fold_in(key_of[2], 71), 0),
        "coefficients": normal_values(key_of[1], (SAMPLES,), 1.0, 6.0, ((0, 16),), jnp.float32),
    }


def reference(log_derivs, coefficients):
    column_mean = lax.optimization_barrier(jnp.sum(log_derivs, axis=0)) / SAMPLES
    centred = (log_derivs - column_mean[None, :]) / jnp.sqrt(jnp.float32(SAMPLES))
    gram = jnp.dot(centred, centred.T, precision=lax.Precision.HIGHEST, preferred_element_type=jnp.float32)
    update = jnp.dot(coefficients, centred, precision=lax.Precision.HIGHEST, preferred_element_type=jnp.float32)
    return (gram, update)
```

```python
import functools

import jax
import jax.numpy as jnp
from jax import lax
from jax.experimental import pallas as pl
from jax.experimental.pallas import tpu as pltpu
from jax.sharding import PartitionSpec as P

BOTH = ("smp", "par")
VMEM_LIMIT = 40 * 1024 * 1024


def row_products(left_rows, right_rows):
    return lax.dot_general(
        left_rows,
        right_rows,
        (((1,), (1,)), ((), ())),
        precision=lax.Precision.HIGHEST,
        preferred_element_type=jnp.float32,
    )


def gathered(log_derivs, coefficients):
    samples = log_derivs.shape[0] * lax.axis_size("smp")
    column_total = lax.psum(jnp.sum(log_derivs, axis=0), "smp")
    centred = (log_derivs - column_total[None, :] / samples) / jnp.sqrt(jnp.float32(samples))
    partial_gram = row_products(centred, lax.all_gather(centred, "smp", axis=0, tiled=True))
    gram = lax.psum_scatter(partial_gram, "par", scatter_dimension=1, tiled=True)
    update_term = lax.dot_general(
        coefficients,
        centred,
        (((0,), (0,)), ((), ())),
        precision=lax.Precision.HIGHEST,
        preferred_element_type=jnp.float32,
    )
    update = lax.psum_scatter(update_term, "smp", scatter_dimension=0, tiled=True)
    return (gram, update)


def stats_kernel(rows_ref, coef_ref, stats_ref):
    rows = rows_ref[...]
    coef = coef_ref[...]
    mean = jnp.sum(rows, axis=0, keepdims=True) / rows.shape[0]
    stats_ref[0:1, :] = mean
    stats_ref[1:2, :] = jnp.sum(coef * (rows - mean), axis=0, keepdims=True)
    stats_ref[2:3, :] = jnp.broadcast_to(jnp.sum(coef, axis=0, keepdims=True), mean.shape)


def block_stats(rows, coefficients):
    return pl.pallas_call(
        stats_kernel,
        out_shape=jax.ShapeDtypeStruct((8, rows.shape[1]), jnp.float32),
        compiler_params=pltpu.CompilerParams(vmem_limit_bytes=VMEM_LIMIT),
        name="block_stats",
    )(rows, coefficients[:, None])


def merge(*parts):
    mean = sum(p[0:1] for p in parts) / len(parts)
    product = sum(p[1:2] + p[2:3] * (p[0:1] - mean) for p in parts)
    total = sum(p[2:3] for p in parts)
    return jnp.concatenate([mean, product, total, jnp.zeros((5, mean.shape[1]), jnp.float32)], axis=0)


def split(values):
    high = values.astype(jnp.bfloat16)
    return high, (values - high.astype(jnp.float32)).astype(jnp.bfloat16)


def dot_nt(left, right):
    return lax.dot_general(left, right, (((1,), (1,)), ((), ())), preferred_element_type=jnp.float32)


def products_kernel(scale, counts, flag_ref, mean_ref, own_ref, side_ref, *refs):
    first, second = refs[: counts[0]], refs[counts[0] : sum(counts)]
    keep_own, keep_side, *sent = refs[sum(counts) :]
    height = own_ref.shape[0]
    if len(sent) == 1:
        sent = [sent[0].at[pl.ds(0, height)], sent[0].at[pl.ds(height, height)]]
    mean = mean_ref[0:1, :]
    rows = [split(ref[...] - mean) for ref in (own_ref, side_ref)]

    def fill(column_refs, outs):
        at = 0
        for ref in column_refs:
            high, low = split(ref[...] - mean)
            width = ref.shape[0]
            for (row_high, row_low), out in zip(rows, outs):
                total = dot_nt(row_high, high) + (dot_nt(row_high, low) + dot_nt(row_low, high))
                out[:, at : at + width] = total * scale
            at += width

    @pl.when(flag_ref[0] == 1)
    def _():
        fill(first, (keep_own, keep_side))
        fill(second, sent)

    @pl.when(flag_ref[0] != 1)
    def _():
        fill(second, (keep_own, keep_side))
        fill(first, sent)


def products(mean, own, side, flag, first, second, samples, joined, name):
    rows, params = own.shape
    width = sum(block.shape[0] for block in first)
    out = jax.ShapeDtypeStruct((rows, width), jnp.float32)
    both = jax.ShapeDtypeStruct((2 * rows, width), jnp.float32)
    return pl.pallas_call(
        functools.partial(products_kernel, 1.0 / samples, (len(first), len(second))),
        out_shape=(out, out, both) if joined else (out, out, out, out),
        in_specs=[pl.BlockSpec(memory_space=pltpu.SMEM)]
        + [pl.BlockSpec(memory_space=pltpu.VMEM)] * (3 + len(first) + len(second)),
        compiler_params=pltpu.CompilerParams(vmem_limit_bytes=VMEM_LIMIT),
        cost_estimate=pl.CostEstimate(
            flops=24 * rows * width * params, bytes_accessed=16 * (rows + width) * params, transcendentals=0
        ),
        name=name,
    )(flag, mean, own, side, *first, *second)


def place_kernel(summands, splits, aliased, at_ref, *refs):
    blocks = list(refs[: sum(summands)])
    out = refs[len(blocks) + aliased]
    *totals, sems = refs[len(blocks) + aliased + 1 :]
    copies = []
    for total, terms, parts in zip(totals, summands, splits):
        taken, blocks = blocks[:terms], blocks[terms:]
        value = taken[0][0 : total.shape[0], :]
        for block in taken[1:]:
            value += block[0 : total.shape[0], :]
        total[...] = value
        width = total.shape[1] // parts
        for part in range(parts):
            at = pl.multiple_of(at_ref[len(copies)] * 128, 128)
            copy = pltpu.make_async_copy(
                total.at[:, pl.ds(part * width, width)], out.at[:, pl.ds(at, width)], sems.at[len(copies)]
            )
            copy.start()
            copies.append(copy)
    for copy in copies:
        copy.wait()


def place(pieces, shape, into, name):
    blocks = [block for terms, _ in pieces for block in terms]
    at = jnp.stack([column for _, columns in pieces for column in columns]).astype(jnp.int32)
    aliased = 0 if into is None else 1
    return pl.pallas_call(
        functools.partial(
            place_kernel, [len(terms) for terms, _ in pieces], [len(columns) for _, columns in pieces], aliased
        ),
        out_shape=jax.ShapeDtypeStruct(shape, jnp.float32),
        in_specs=[pl.BlockSpec(memory_space=pltpu.SMEM)]
        + [pl.BlockSpec(memory_space=pltpu.VMEM)] * len(blocks)
        + [pl.BlockSpec(memory_space=pl.ANY)] * aliased,
        out_specs=pl.BlockSpec(memory_space=pl.ANY),
        scratch_shapes=[pltpu.VMEM((shape[0], terms[0].shape[1]), jnp.float32) for terms, _ in pieces]
        + [pltpu.SemaphoreType.DMA((at.shape[0],))],
        input_output_aliases={1 + len(blocks): 0} if aliased else {},
        compiler_params=pltpu.CompilerParams(vmem_limit_bytes=VMEM_LIMIT),
        name=name,
    )(at, *blocks, *([into] if aliased else []))


def ringed(log_derivs, coefficients):
    rows, params = log_derivs.shape
    samples = rows * lax.axis_size("smp")
    levels, planes = lax.axis_size("smp") // 4, lax.axis_size("par")
    per_plane = levels // planes
    here, plane = lax.axis_index("smp"), lax.axis_index("par")
    level, side, core = here // 4, (here // 2) % 2, here % 2
    half = rows // 2

    def moves(to):
        pairs = []
        for z in range(levels):
            for x in range(2):
                for c in range(2):
                    for y in range(planes):
                        tz, tx, tc, ty = to(z, x, c, y)
                        target = ((tz % levels) * 2 + tx) * 2 + tc
                        pairs.append((((z * 2 + x) * 2 + c) * planes + y, target * planes + ty))
        return pairs

    ring = moves(lambda z, x, c, y: (z + 1 - 2 * c, x, c, y))
    over_side = moves(lambda z, x, c, y: (z, 1 - x, c, y))
    over_core = moves(lambda z, x, c, y: (z, x, 1 - c, y))
    over_plane = moves(lambda z, x, c, y: (z, x, c, 1 - y))
    diagonal = moves(lambda z, x, c, y: (z, 1 - x, c, 1 - y))
    turns = [moves(lambda z, x, c, y, k=k: (z + k, x, c, y)) for k in range(1, levels)]

    def send(value, pairs):
        return lax.ppermute(value, BOTH, pairs)

    one = [send(part, ring) for part in (log_derivs[:half], log_derivs[half:])]

    stats = block_stats(log_derivs, coefficients)
    stats = merge(stats, send(stats, over_core))
    stats = merge(stats, send(stats, over_side))
    stats = merge(stats, *[send(stats, turn) for turn in turns])
    share = params // lax.axis_size("smp")
    update = lax.dynamic_slice(stats, (1, here * share), (1, share))[0] / jnp.sqrt(jnp.float32(samples))

    side_rows = send(log_derivs, over_side)
    core_rows = send(log_derivs, over_core)
    two = [send(part, ring) for part in one]
    one_core = [send(part, over_core) for part in one]
    three = [send(part, ring) for part in two]
    two_core = [send(part, over_core) for part in two]
    three_core = [send(part, over_core) for part in three]

    near = (level - 1 + 2 * core + levels) % levels
    far = (level + 1 - 2 * core + levels) % levels
    across = (level + levels // 2) % levels

    def kept(z):
        return z // per_plane == plane

    def column(z, x, c, part=0):
        return (((z % per_plane) * 2 + x) * 2 + c) * (rows // 128) + part * (half // 128)

    product = functools.partial(products, stats, log_derivs, side_rows, samples=samples)
    shape = (rows, rows * 4 * per_plane)

    keep_own, keep_side, sent = product(
        kept(near).astype(jnp.int32)[None], one, one_core, joined=True, name="products_one"
    )
    got = send(sent, over_plane)
    from_side = send(keep_side + got[rows:], over_side)
    z = jnp.where(kept(near), near, far)
    c = jnp.where(kept(near), core, 1 - core)
    pieces = [((keep_own, got), [column(z, side, c)]), ((from_side,), [column(z, 1 - side, c)])]

    keep_own, keep_side, sent = product(
        kept(level).astype(jnp.int32)[None],
        [log_derivs, core_rows],
        [*two, *two_core],
        joined=True,
        name="products_two",
    )
    got = send(sent, over_plane)
    from_side = send(keep_side + got[rows:], over_side)
    z = jnp.where(kept(level), level, across)
    pieces += [
        ((keep_own, got), [column(z, side, core), column(z, side, 1 - core)]),
        ((from_side,), [column(z, 1 - side, core), column(z, 1 - side, 1 - core)]),
    ]
    gram = place(pieces, shape, None, "place_most")

    z = jnp.where(kept(far), far, near)
    c = jnp.where(kept(far), core, 1 - core)
    pieces = []
    for part in range(2):
        keep_own, keep_side, send_own, send_side = product(
            kept(far).astype(jnp.int32)[None],
            [three[part]],
            [three_core[part]],
            joined=False,
            name="products_three",
        )
        got_own = send(send_own, over_plane)
        got_side = send(send_side, diagonal)
        from_side = send(keep_side, over_side)
        pieces += [
            ((keep_own, got_own), [column(z, side, c, part)]),
            ((from_side, got_side), [column(z, 1 - side, c, part)]),
        ]
    return (place(pieces, shape, gram, "place_last"), update)


def solution(mesh):
    placed = (P("smp", "par"), P("smp"))
    levels, planes = mesh.shape["smp"] // 4, mesh.shape["par"]
    return jax.shard_map(
        ringed if planes == 2 and levels == 2 * planes else gathered,
        mesh=mesh,
        in_specs=placed,
        out_specs=(P("smp", "par"), P(("par", "smp"))),
        check_vma=False,
    )
```

```python
import functools

import jax
import jax.numpy as jnp
import numpy as np
from jax import lax
from jax.experimental import pallas as pl
from jax.experimental.pallas import tpu as pltpu
from jax.sharding import PartitionSpec as P

BOTH = ("smp", "par")
VMEM_LIMIT = 24 * 1024 * 1024
FREE = pl.CostEstimate(flops=0, bytes_accessed=0, transcendentals=0)


def row_products(left_rows, right_rows):
    return lax.dot_general(
        left_rows,
        right_rows,
        (((1,), (1,)), ((), ())),
        precision=lax.Precision.HIGHEST,
        preferred_element_type=jnp.float32,
    )


def gathered(log_derivs, coefficients):
    samples = log_derivs.shape[0] * lax.axis_size("smp")
    column_total = lax.psum(jnp.sum(log_derivs, axis=0), "smp")
    centred = (log_derivs - column_total[None, :] / samples) / jnp.sqrt(jnp.float32(samples))
    partial_gram = row_products(centred, lax.all_gather(centred, "smp", axis=0, tiled=True))
    gram = lax.psum_scatter(partial_gram, "par", scatter_dimension=1, tiled=True)
    update_term = lax.dot_general(
        coefficients,
        centred,
        (((0,), (0,)), ((), ())),
        precision=lax.Precision.HIGHEST,
        preferred_element_type=jnp.float32,
    )
    update = lax.psum_scatter(update_term, "smp", scatter_dimension=0, tiled=True)
    return (gram, update)


def after(value, *others):
    return lax.optimization_barrier((value, *others))[0]


def stats_kernel(rows_ref, coef_ref, stats_ref):
    rows = rows_ref[...]
    mean = jnp.sum(rows, axis=0, keepdims=True) / rows.shape[0]
    stats_ref[0:1, :] = mean
    stats_ref[1:2, :] = jnp.dot(
        coef_ref[...], rows - mean, precision=lax.Precision.HIGHEST, preferred_element_type=jnp.float32
    )
    stats_ref[2:3, :] = jnp.broadcast_to(jnp.sum(coef_ref[...], axis=1, keepdims=True), mean.shape)
    stats_ref[3:, :] = jnp.zeros((stats_ref.shape[0] - 3, mean.shape[1]), jnp.float32)


def block_stats(rows, coefficients):
    return pl.pallas_call(
        stats_kernel,
        out_shape=jax.ShapeDtypeStruct((8, rows.shape[1]), jnp.float32),
        compiler_params=pltpu.CompilerParams(vmem_limit_bytes=VMEM_LIMIT),
        cost_estimate=FREE,
        name="block_stats",
    )(rows, coefficients[None, :])


def merge_kernel(count, *refs):
    parts, out = refs[:count], refs[count]
    mean = sum(p[0:1, :] for p in parts) / count
    out[...] = jnp.zeros_like(out)
    out[0:1, :] = mean
    out[1:2, :] = sum(p[1:2, :] + p[2:3, :] * (p[0:1, :] - mean) for p in parts)
    out[2:3, :] = sum(p[2:3, :] for p in parts)


def merge(*parts):
    return kernel_call(functools.partial(merge_kernel, len(parts)), [parts[0].shape], "merge", *parts)[0]


def split(values):
    high = values.astype(jnp.bfloat16)
    return high, (values - high.astype(jnp.float32)).astype(jnp.bfloat16)


def dot_nt(left, right):
    return lax.dot_general(left, right, (((1,), (1,)), ((), ())), preferred_element_type=jnp.float32)


def device_row(planes):
    return lax.axis_index("smp") * planes + lax.axis_index("par")


def product_of(row_ref, mean, high, low, scale):
    row_high, row_low = split(row_ref[...] - mean)
    return (dot_nt(row_high, high) + (dot_nt(row_high, low) + dot_nt(row_low, high))) * scale


def one_level_kernel(scale, mean_ref, *refs):
    rows, block, outs = refs[:4], refs[4], refs[5:]
    mean = mean_ref[0:1, :]
    high, low = split(block[...] - mean)
    straight = lax.axis_index("par") == 0
    for side in range(2):
        same = product_of(rows[2 * side], mean, high, low, scale)
        other = product_of(rows[2 * side + 1], mean, high, low, scale)
        outs[2 * side][...] = jnp.where(straight, same, other)
        outs[2 * side + 1][...] = jnp.where(straight, other, same)


def two_levels_kernel(scale, planes, flag_at, table_ref, mean_ref, *refs):
    rows, blocks, outs = refs[:4], refs[4:6], refs[6:]
    mean = mean_ref[0:1, :]
    first = table_ref[device_row(planes), flag_at] == 1
    high, low = split(jnp.concatenate([block[...] for block in blocks], axis=0) - mean)
    height, width = rows[0].shape[0], blocks[0].shape[0]
    for k, row in enumerate(rows):
        total = product_of(row, mean, high, low, scale)
        one, other = total[:, :width], total[:, width:]
        place = slice(k % 2 * height, (k % 2 + 1) * height)
        outs[k // 2][place, :] = jnp.where(first, one, other)
        outs[2 + k // 2][place, :] = jnp.where(first, other, one)


def across_kernel(keep_own, got_own, from_side, got_side, own, side):
    height = own.shape[0]
    own[...] = keep_own[height:, :] + got_own[height:, :]
    side[...] = from_side[height:, :] + got_side[height:, :]


def kernel_call(kernel, out_shapes, name, *args, smem=0):
    return pl.pallas_call(
        kernel,
        out_shape=[jax.ShapeDtypeStruct(s, jnp.float32) for s in out_shapes],
        in_specs=[pl.BlockSpec(memory_space=pltpu.SMEM)] * smem
        + [pl.BlockSpec(memory_space=pltpu.VMEM)] * (len(args) - smem),
        out_specs=[pl.BlockSpec(memory_space=pltpu.VMEM)] * len(out_shapes),
        compiler_params=pltpu.CompilerParams(vmem_limit_bytes=VMEM_LIMIT),
        cost_estimate=FREE,
        name=name,
    )(*args)


def place_kernel(planes, summands, columns, aliased, table_ref, *refs):
    blocks = list(refs[: sum(summands)])
    out = refs[len(blocks) + aliased]
    *totals, sems = refs[len(blocks) + aliased + 1 :]
    row = device_row(planes)
    stores = []
    for total, terms, places in zip(totals, summands, columns):
        taken, blocks = blocks[:terms], blocks[terms:]
        if terms > 1:
            total[...] = taken[0][0 : total.shape[0], :] + taken[1][0 : total.shape[0], :]
        else:
            total = taken[0]
        width = total.shape[1] // len(places)
        for part, (where, offset) in enumerate(places):
            column = pl.multiple_of((table_ref[row, where] + offset) * 128, 128)
            stores.append(
                pltpu.make_async_copy(
                    total.at[:, pl.ds(part * width, width)], out.at[:, pl.ds(column, width)], sems.at[len(stores)]
                )
            )
            stores[-1].start()
    for store in stores:
        store.wait()


def place(table, planes, pieces, shape, into, name):
    blocks = [block for terms, _ in pieces for block in terms]
    columns = [places for _, places in pieces]
    aliased = 0 if into is None else 1
    near, far = pl.BlockSpec(memory_space=pltpu.VMEM), pl.BlockSpec(memory_space=pl.ANY)
    return pl.pallas_call(
        functools.partial(place_kernel, planes, [len(terms) for terms, _ in pieces], columns, aliased),
        out_shape=jax.ShapeDtypeStruct(shape, jnp.float32),
        in_specs=[pl.BlockSpec(memory_space=pltpu.SMEM)] + [near] * len(blocks) + [far] * aliased,
        out_specs=far,
        scratch_shapes=[pltpu.VMEM((shape[0], terms[0].shape[1]), jnp.float32) for terms, _ in pieces]
        + [pltpu.SemaphoreType.DMA((sum(map(len, columns)),))],
        input_output_aliases={1 + len(blocks): 0} if aliased else {},
        compiler_params=pltpu.CompilerParams(vmem_limit_bytes=VMEM_LIMIT),
        cost_estimate=FREE,
        name=name,
    )(table, *blocks, *([into] if aliased else []))


def column_table(levels, planes, block):
    per_plane = levels // planes
    table = np.zeros((levels * 4 * planes, 16), np.int32)

    def column(level, side, core):
        return ((level % per_plane * 2 + side) * 2 + core) * block

    for z in range(levels):
        for x in range(2):
            for c in range(2):
                for y in range(planes):
                    row = [int(z // per_plane == y)]
                    for step in (-1, 1):
                        for core in range(2):
                            level = (z + step * (1 - 2 * core)) % levels
                            if level // per_plane == y:
                                row += [column(level, x, core), column(level, 1 - x, core)]
                    level = z if row[0] else (z + levels // 2) % levels
                    for core in (c, 1 - c):
                        row += [column(level, x, core), column(level, 1 - x, core)]
                    table[((z * 2 + x) * 2 + c) * planes + y, : len(row)] = row
    return table


def ringed(log_derivs, coefficients):
    rows, params = log_derivs.shape
    samples = rows * lax.axis_size("smp")
    levels, planes = lax.axis_size("smp") // 4, lax.axis_size("par")
    per_plane = levels // planes
    shape = (rows, rows * 4 * per_plane)
    scale = 1.0 / samples

    def moves(to):
        pairs = []
        for z in range(levels):
            for x in range(2):
                for c in range(2):
                    for y in range(planes):
                        tz, tx, tc, ty = to(z, x, c, y)
                        target = ((tz % levels) * 2 + tx) * 2 + tc
                        pairs.append((((z * 2 + x) * 2 + c) * planes + y, target * planes + ty))
        return pairs

    def holder(z):
        return z % levels // per_plane

    ring = moves(lambda z, x, c, y: (z + 1 - 2 * c, x, c, y))
    over_core = moves(lambda z, x, c, y: (z, x, 1 - c, y))
    over_side = moves(lambda z, x, c, y: (z, 1 - x, c, y))
    over_both = moves(lambda z, x, c, y: (z, 1 - x, 1 - c, y))
    over_plane = moves(lambda z, x, c, y: (z, x, c, 1 - y))
    diagonal = moves(lambda z, x, c, y: (z, 1 - x, c, 1 - y))
    turns = [moves(lambda z, x, c, y, k=k: (z + k, x, c, y)) for k in range(1, levels)]

    def to_holder(step, side, swap):
        return moves(lambda z, x, c, y: (z, x ^ side, c ^ y ^ swap, holder(z - step * (1 - 2 * c))))

    def send(value, pairs):
        return lax.ppermute(value, BOTH, pairs)

    table = jnp.asarray(column_table(levels, planes, rows // 128))

    core_rows = send(log_derivs, over_core)
    one = send(log_derivs, ring)

    side_rows = send(log_derivs, over_side)

    stats = block_stats(log_derivs, coefficients)
    stats = merge(stats, *[send(stats, turn) for turn in turns])
    one, side_rows = lax.optimization_barrier((one, side_rows, stats))[:2]
    two = send(one, ring)
    stats = merge(stats, send(stats, over_core), send(stats, over_side), send(stats, over_both))
    side_core_rows = send(side_rows, over_core)
    all_rows = (log_derivs, core_rows, side_rows, side_core_rows)

    def one_level(block, step, name):
        out = kernel_call(functools.partial(one_level_kernel, scale), [(rows, rows)] * 4, name, stats, *all_rows, block)
        sent = [send(out[2 * side + swap], to_holder(step, side, swap)) for side in range(2) for swap in range(2)]
        return out, (sent[:2], sent[2:])

    out, near = one_level(one, 1, "products_near")
    share = params // lax.axis_size("smp")

    two = after(two, *near[0], *near[1])
    three = send(two, ring)
    keep_own, keep_side, sent_own, sent_side = kernel_call(
        functools.partial(two_levels_kernel, scale, planes, 0),
        [(2 * rows, rows)] * 4,
        "products_across",
        table,
        stats,
        *all_rows,
        log_derivs,
        two,
        smem=1,
    )
    got_own = send(sent_own, over_plane)
    got_side = send(sent_side, diagonal)
    from_side = send(keep_side, over_side)

    out, far = one_level(three, -1, "products_far")

    got_own = after(got_own, out[0])
    own, side = kernel_call(across_kernel, [(rows, rows)] * 2, "sum_across", keep_own, got_own, from_side, got_side)
    across_own, across_side = send(own, over_core), send(side, over_core)
    update = lax.dynamic_slice(after(stats, out[0]), (1, lax.axis_index("smp") * share), (1, share))[0]
    update = update / jnp.sqrt(jnp.float32(samples))
    gram = place(
        table,
        planes,
        [(near[0], [(1, 0)]), (near[1], [(2, 0)]), ((keep_own, got_own), [(5, 0)]), ((from_side, got_side), [(6, 0)])],
        shape,
        None,
        "place_most",
    )
    gram = after(gram, *far[0], *far[1])
    gram = place(
        table,
        planes,
        [(far[0], [(3, 0)]), (far[1], [(4, 0)]), ((across_own,), [(7, 0)]), ((across_side,), [(8, 0)])],
        shape,
        gram,
        "place_last",
    )
    return (gram, update)


def solution(mesh):
    placed = (P("smp", "par"), P("smp"))
    levels, planes = mesh.shape["smp"] // 4, mesh.shape["par"]
    return jax.shard_map(
        ringed if planes == 2 and levels == 2 * planes else gathered,
        mesh=mesh,
        in_specs=placed,
        out_specs=(P("smp", "par"), P(("par", "smp"))),
        check_vma=False,
    )
```

```python
import functools

import jax
import jax.numpy as jnp
import numpy as np
from jax import lax
from jax.experimental import pallas as pl
from jax.experimental.pallas import tpu as pltpu
from jax.sharding import PartitionSpec as P

BOTH = ("smp", "par")
VMEM_LIMIT = 16 * 1024 * 1024
FREE = pl.CostEstimate(flops=0, bytes_accessed=0, transcendentals=0)


def row_products(left_rows, right_rows):
    return lax.dot_general(
        left_rows,
        right_rows,
        (((1,), (1,)), ((), ())),
        precision=lax.Precision.HIGHEST,
        preferred_element_type=jnp.float32,
    )


def gathered(log_derivs, coefficients):
    samples = log_derivs.shape[0] * lax.axis_size("smp")
    column_total = lax.psum(jnp.sum(log_derivs, axis=0), "smp")
    centred = (log_derivs - column_total[None, :] / samples) / jnp.sqrt(jnp.float32(samples))
    partial_gram = row_products(centred, lax.all_gather(centred, "smp", axis=0, tiled=True))
    gram = lax.psum_scatter(partial_gram, "par", scatter_dimension=1, tiled=True)
    update_term = lax.dot_general(
        coefficients,
        centred,
        (((0,), (0,)), ((), ())),
        precision=lax.Precision.HIGHEST,
        preferred_element_type=jnp.float32,
    )
    update = lax.psum_scatter(update_term, "smp", scatter_dimension=0, tiled=True)
    return (gram, update)


def after(value, *others):
    return lax.optimization_barrier((value, *others))[0]


def stats_kernel(rows_ref, other_ref, coef_ref, other_coef_ref, stats_ref):
    blocks = (rows_ref, other_ref)
    mean = sum(jnp.sum(ref[...], axis=0, keepdims=True) for ref in blocks) / sum(ref.shape[0] for ref in blocks)
    stats_ref[...] = jnp.zeros_like(stats_ref)
    stats_ref[0:1, :] = mean
    stats_ref[1:2, :] = sum(
        jnp.dot(coef[...], ref[...] - mean, precision=lax.Precision.HIGHEST, preferred_element_type=jnp.float32)
        for coef, ref in zip((coef_ref, other_coef_ref), blocks)
    )
    total = sum(jnp.sum(coef[...], axis=1, keepdims=True) for coef in (coef_ref, other_coef_ref))
    stats_ref[2:3, :] = jnp.broadcast_to(total, mean.shape)


def block_stats(rows, other, coefficients, other_coefficients):
    return kernel_call(
        stats_kernel, [(8, rows.shape[1])], "block_stats", rows, other, coefficients, other_coefficients
    )[0]


def merge_kernel(count, *refs):
    parts, out = refs[:count], refs[count]
    mean = sum(p[0:1, :] for p in parts) / count
    out[...] = jnp.zeros_like(out)
    out[0:1, :] = mean
    out[1:2, :] = sum(p[1:2, :] + p[2:3, :] * (p[0:1, :] - mean) for p in parts)
    out[2:3, :] = sum(p[2:3, :] for p in parts)


def merge(*parts):
    return kernel_call(functools.partial(merge_kernel, len(parts)), [parts[0].shape], "merge", *parts)[0]


def split(values):
    high = values.astype(jnp.bfloat16)
    return high, (values - high.astype(jnp.float32)).astype(jnp.bfloat16)


def dot_nt(left, right):
    return lax.dot_general(left, right, (((1,), (1,)), ((), ())), preferred_element_type=jnp.float32)


def device_row(planes):
    return lax.axis_index("smp") * planes + lax.axis_index("par")


def product_of(row_ref, mean, high, low, scale):
    row_high, row_low = split(row_ref[...] - mean)
    return (dot_nt(row_high, high) + (dot_nt(row_high, low) + dot_nt(row_low, high))) * scale


def one_level_kernel(scale, mean_ref, *refs):
    rows, block, outs = refs[:4], refs[4], refs[5:]
    mean = mean_ref[0:1, :]
    high, low = split(block[...] - mean)
    straight = lax.axis_index("par") == 0
    for side in range(2):
        same = product_of(rows[2 * side], mean, high, low, scale)
        other = product_of(rows[2 * side + 1], mean, high, low, scale)
        outs[2 * side][...] = jnp.where(straight, same, other)
        outs[2 * side + 1][...] = jnp.where(straight, other, same)


def own_level_kernel(scale, mean_ref, *refs):
    rows, block, outs = refs[:4], refs[4], refs[5:]
    mean = mean_ref[0:1, :]
    high, low = split(block[...] - mean)
    height = rows[0].shape[0]
    for k, row in enumerate(rows):
        outs[k // 2][k % 2 * height : (k % 2 + 1) * height, :] = product_of(row, mean, high, low, scale)


def across_level_kernel(scale, planes, flag_at, table_ref, mean_ref, *refs):
    rows, block, level, outs = refs[:4], refs[4], refs[5:7], refs[7:]
    mean = mean_ref[0:1, :]
    first = table_ref[device_row(planes), flag_at] == 1
    high, low = split(block[...] - mean)
    height = rows[0].shape[0]
    for k, row in enumerate(rows):
        total = product_of(row, mean, high, low, scale)
        place = slice(k % 2 * height, (k % 2 + 1) * height)
        here = level[k // 2][place, :]
        outs[k // 2][place, :] = jnp.where(first, here, total)
        outs[2 + k // 2][place, :] = jnp.where(first, total, here)


def across_kernel(keep_own, got_own, from_side, got_side, own, side):
    height = own.shape[0]
    own[...] = keep_own[height:, :] + got_own[height:, :]
    side[...] = from_side[height:, :] + got_side[height:, :]


def kernel_call(kernel, out_shapes, name, *args, smem=0):
    return pl.pallas_call(
        kernel,
        out_shape=[jax.ShapeDtypeStruct(s, jnp.float32) for s in out_shapes],
        in_specs=[pl.BlockSpec(memory_space=pltpu.SMEM)] * smem
        + [pl.BlockSpec(memory_space=pltpu.VMEM)] * (len(args) - smem),
        out_specs=[pl.BlockSpec(memory_space=pltpu.VMEM)] * len(out_shapes),
        compiler_params=pltpu.CompilerParams(vmem_limit_bytes=VMEM_LIMIT),
        cost_estimate=FREE,
        name=name,
    )(*args)


def place_kernel(planes, summands, columns, aliased, table_ref, *refs):
    blocks = list(refs[: sum(summands)])
    out = refs[len(blocks) + aliased]
    *totals, sems = refs[len(blocks) + aliased + 1 :]
    row = device_row(planes)
    stores = []
    for total, terms, places in zip(totals, summands, columns):
        taken, blocks = blocks[:terms], blocks[terms:]
        if terms > 1:
            total[...] = taken[0][0 : total.shape[0], :] + taken[1][0 : total.shape[0], :]
        else:
            total = taken[0]
        width = total.shape[1] // len(places)
        for part, (where, offset) in enumerate(places):
            column = pl.multiple_of((table_ref[row, where] + offset) * 128, 128)
            stores.append(
                pltpu.make_async_copy(
                    total.at[:, pl.ds(part * width, width)], out.at[:, pl.ds(column, width)], sems.at[len(stores)]
                )
            )
            stores[-1].start()
    for store in stores:
        store.wait()


def place(table, planes, pieces, shape, into, name):
    blocks = [block for terms, _ in pieces for block in terms]
    columns = [places for _, places in pieces]
    aliased = 0 if into is None else 1
    near, far = pl.BlockSpec(memory_space=pltpu.VMEM), pl.BlockSpec(memory_space=pl.ANY)
    return pl.pallas_call(
        functools.partial(place_kernel, planes, [len(terms) for terms, _ in pieces], columns, aliased),
        out_shape=jax.ShapeDtypeStruct(shape, jnp.float32),
        in_specs=[pl.BlockSpec(memory_space=pltpu.SMEM)] + [near] * len(blocks) + [far] * aliased,
        out_specs=far,
        scratch_shapes=[pltpu.VMEM((shape[0], terms[0].shape[1]), jnp.float32) for terms, _ in pieces]
        + [pltpu.SemaphoreType.DMA((sum(map(len, columns)),))],
        input_output_aliases={1 + len(blocks): 0} if aliased else {},
        compiler_params=pltpu.CompilerParams(vmem_limit_bytes=VMEM_LIMIT),
        cost_estimate=FREE,
        name=name,
    )(table, *blocks, *([into] if aliased else []))


def column_table(levels, planes, block):
    per_plane = levels // planes
    table = np.zeros((levels * 4 * planes, 16), np.int32)

    def column(level, side, core):
        return ((level % per_plane * 2 + side) * 2 + core) * block

    for z in range(levels):
        for x in range(2):
            for c in range(2):
                for y in range(planes):
                    row = [int(z // per_plane == y)]
                    for step in (-1, 1):
                        for core in range(2):
                            level = (z + step * (1 - 2 * core)) % levels
                            if level // per_plane == y:
                                row += [column(level, x, core), column(level, 1 - x, core)]
                    level = z if row[0] else (z + levels // 2) % levels
                    for core in (c, 1 - c):
                        row += [column(level, x, core), column(level, 1 - x, core)]
                    table[((z * 2 + x) * 2 + c) * planes + y, : len(row)] = row
    return table


def ringed(log_derivs, coefficients):
    rows, params = log_derivs.shape
    samples = rows * lax.axis_size("smp")
    levels, planes = lax.axis_size("smp") // 4, lax.axis_size("par")
    per_plane = levels // planes
    shape = (rows, rows * 4 * per_plane)
    scale = 1.0 / samples

    def moves(to):
        pairs = []
        for z in range(levels):
            for x in range(2):
                for c in range(2):
                    for y in range(planes):
                        tz, tx, tc, ty = to(z, x, c, y)
                        target = ((tz % levels) * 2 + tx) * 2 + tc
                        pairs.append((((z * 2 + x) * 2 + c) * planes + y, target * planes + ty))
        return pairs

    def holder(z):
        return z % levels // per_plane

    ring = moves(lambda z, x, c, y: (z + 1 - 2 * c, x, c, y))
    over_core = moves(lambda z, x, c, y: (z, x, 1 - c, y))
    over_side = moves(lambda z, x, c, y: (z, 1 - x, c, y))
    over_plane = moves(lambda z, x, c, y: (z, x, c, 1 - y))
    diagonal = moves(lambda z, x, c, y: (z, 1 - x, c, 1 - y))
    turns = [moves(lambda z, x, c, y, k=k: (z + k, x, c, y)) for k in range(1, levels)]

    def to_holder(step, side, swap):
        return moves(lambda z, x, c, y: (z, x ^ side, c ^ y ^ swap, holder(z - step * (1 - 2 * c))))

    def send(value, pairs):
        return lax.ppermute(value, BOTH, pairs)

    table = jnp.asarray(column_table(levels, planes, rows // 128))

    core_rows = send(log_derivs, over_core)
    one = send(log_derivs, ring)

    side_rows = send(log_derivs, over_side)

    coefficients = coefficients[None, :]
    stats = block_stats(log_derivs, core_rows, coefficients, send(coefficients, over_core))
    stats = merge(stats, *[send(stats, turn) for turn in turns])
    one, side_rows = lax.optimization_barrier((one, side_rows, stats))[:2]
    two = send(one, ring)
    stats = merge(stats, send(stats, over_side))
    side_core_rows = send(side_rows, over_core)
    all_rows = (log_derivs, core_rows, side_rows, side_core_rows)

    def one_level(block, step, name):
        out = kernel_call(functools.partial(one_level_kernel, scale), [(rows, rows)] * 4, name, stats, *all_rows, block)
        sent = [send(out[2 * side + swap], to_holder(step, side, swap)) for side in range(2) for swap in range(2)]
        return out, (sent[:2], sent[2:])

    out, near = one_level(one, 1, "products_near")
    share = params // lax.axis_size("smp")

    own_level = kernel_call(
        functools.partial(own_level_kernel, scale),
        [(2 * rows, rows)] * 2,
        "products_level",
        stats,
        *all_rows,
        after(log_derivs, out[0]),
    )
    two = after(two, *near[0], *near[1], *own_level)
    three = send(two, ring)
    keep_own, keep_side, sent_own, sent_side = kernel_call(
        functools.partial(across_level_kernel, scale, planes, 0),
        [(2 * rows, rows)] * 4,
        "products_across",
        table,
        stats,
        *all_rows,
        two,
        *own_level,
        smem=1,
    )
    got_own = send(sent_own, over_plane)
    got_side = send(sent_side, diagonal)
    from_side = send(keep_side, over_side)

    out, far = one_level(three, -1, "products_far")

    got_own = after(got_own, out[0])
    own, side = kernel_call(across_kernel, [(rows, rows)] * 2, "sum_across", keep_own, got_own, from_side, got_side)
    across_own, across_side = send(own, over_core), send(side, over_core)
    update = lax.dynamic_slice(after(stats, out[0]), (1, lax.axis_index("smp") * share), (1, share))[0]
    update = update / jnp.sqrt(jnp.float32(samples))
    gram = place(
        table,
        planes,
        [(near[0], [(1, 0)]), (near[1], [(2, 0)]), ((keep_own, got_own), [(5, 0)]), ((from_side, got_side), [(6, 0)])],
        shape,
        None,
        "place_most",
    )
    gram = after(gram, *far[0], *far[1])
    gram = place(
        table,
        planes,
        [(far[0], [(3, 0)]), (far[1], [(4, 0)]), ((across_own,), [(7, 0)]), ((across_side,), [(8, 0)])],
        shape,
        gram,
        "place_last",
    )
    return (gram, update)


def solution(mesh):
    placed = (P("smp", "par"), P("smp"))
    levels, planes = mesh.shape["smp"] // 4, mesh.shape["par"]
    return jax.shard_map(
        ringed if planes == 2 and levels == 2 * planes else gathered,
        mesh=mesh,
        in_specs=placed,
        out_specs=(P("smp", "par"), P(("par", "smp"))),
        check_vma=False,
    )
```

```python
import functools

import jax
import jax.numpy as jnp
import numpy as np
from jax import lax
from jax.experimental import pallas as pl
from jax.experimental.pallas import tpu as pltpu
from jax.sharding import PartitionSpec as P

BOTH = ("smp", "par")
VMEM_LIMIT = 16 * 1024 * 1024
FREE = pl.CostEstimate(flops=0, bytes_accessed=0, transcendentals=0)


def row_products(left_rows, right_rows):
    return lax.dot_general(
        left_rows,
        right_rows,
        (((1,), (1,)), ((), ())),
        precision=lax.Precision.HIGHEST,
        preferred_element_type=jnp.float32,
    )


def gathered(log_derivs, coefficients):
    samples = log_derivs.shape[0] * lax.axis_size("smp")
    column_total = lax.psum(jnp.sum(log_derivs, axis=0), "smp")
    centred = (log_derivs - column_total[None, :] / samples) / jnp.sqrt(jnp.float32(samples))
    partial_gram = row_products(centred, lax.all_gather(centred, "smp", axis=0, tiled=True))
    gram = lax.psum_scatter(partial_gram, "par", scatter_dimension=1, tiled=True)
    update_term = lax.dot_general(
        coefficients,
        centred,
        (((0,), (0,)), ((), ())),
        precision=lax.Precision.HIGHEST,
        preferred_element_type=jnp.float32,
    )
    update = lax.psum_scatter(update_term, "smp", scatter_dimension=0, tiled=True)
    return (gram, update)


def after(value, *others):
    return lax.optimization_barrier((value, *others))[0]


def stats_kernel(rows_ref, other_ref, coef_ref, other_coef_ref, stats_ref):
    blocks = (rows_ref, other_ref)
    mean = sum(jnp.sum(ref[...], axis=0, keepdims=True) for ref in blocks) / sum(ref.shape[0] for ref in blocks)
    stats_ref[...] = jnp.zeros_like(stats_ref)
    stats_ref[0:1, :] = mean
    stats_ref[1:2, :] = sum(
        jnp.dot(coef[...], ref[...] - mean, precision=lax.Precision.HIGHEST, preferred_element_type=jnp.float32)
        for coef, ref in zip((coef_ref, other_coef_ref), blocks)
    )
    total = sum(jnp.sum(coef[...], axis=1, keepdims=True) for coef in (coef_ref, other_coef_ref))
    stats_ref[2:3, :] = jnp.broadcast_to(total, mean.shape)


def block_stats(rows, other, coefficients, other_coefficients):
    return kernel_call(
        stats_kernel, [(8, rows.shape[1])], "block_stats", rows, other, coefficients, other_coefficients
    )[0]


def merge_kernel(count, *refs):
    parts, out = refs[:count], refs[count]
    mean = sum(p[0:1, :] for p in parts) / count
    out[...] = jnp.zeros_like(out)
    out[0:1, :] = mean
    out[1:2, :] = sum(p[1:2, :] + p[2:3, :] * (p[0:1, :] - mean) for p in parts)
    out[2:3, :] = sum(p[2:3, :] for p in parts)


def merge(*parts):
    return kernel_call(functools.partial(merge_kernel, len(parts)), [parts[0].shape], "merge", *parts)[0]


def split(values):
    high = values.astype(jnp.bfloat16)
    return high, (values - high.astype(jnp.float32)).astype(jnp.bfloat16)


def dot_nt(left, right):
    return lax.dot_general(left, right, (((1,), (1,)), ((), ())), preferred_element_type=jnp.float32)


def device_row(planes):
    return lax.axis_index("smp") * planes + lax.axis_index("par")


def product_of(row_ref, mean, high, low, scale):
    row_high, row_low = split(row_ref[...] - mean)
    return (dot_nt(row_high, high) + (dot_nt(row_high, low) + dot_nt(row_low, high))) * scale


def one_level_kernel(scale, mean_ref, *refs):
    rows, block, outs = refs[:4], refs[4], refs[5:]
    mean = mean_ref[0:1, :]
    high, low = split(block[...] - mean)
    straight = lax.axis_index("par") == 0
    for k, side in enumerate((1, 0)):
        same = product_of(rows[2 * side], mean, high, low, scale)
        other = product_of(rows[2 * side + 1], mean, high, low, scale)
        outs[2 * k][...] = jnp.where(straight, same, other)
        outs[2 * k + 1][...] = jnp.where(straight, other, same)


def own_level_kernel(scale, mean_ref, *refs):
    rows, block, outs = refs[:4], refs[4], refs[5:]
    mean = mean_ref[0:1, :]
    high, low = split(block[...] - mean)
    height = rows[0].shape[0]
    for k, row in enumerate(rows):
        outs[k // 2][k % 2 * height : (k % 2 + 1) * height, :] = product_of(row, mean, high, low, scale)


def across_level_kernel(scale, planes, flag_at, table_ref, mean_ref, *refs):
    rows, block, level, outs = refs[:4], refs[4], refs[5:7], refs[7:]
    mean = mean_ref[0:1, :]
    first = table_ref[device_row(planes), flag_at] == 1
    high, low = split(block[...] - mean)
    height = rows[0].shape[0]
    for k, row in enumerate(rows):
        total = product_of(row, mean, high, low, scale)
        place = slice(k % 2 * height, (k % 2 + 1) * height)
        here = level[k // 2][place, :]
        outs[k // 2][place, :] = jnp.where(first, here, total)
        outs[2 + k // 2][place, :] = jnp.where(first, total, here)


def across_kernel(keep_own, got_own, from_side, got_side, own, side):
    height = own.shape[0]
    own[...] = keep_own[height:, :] + got_own[height:, :]
    side[...] = from_side[height:, :] + got_side[height:, :]


def kernel_call(kernel, out_shapes, name, *args, smem=0):
    return pl.pallas_call(
        kernel,
        out_shape=[jax.ShapeDtypeStruct(s, jnp.float32) for s in out_shapes],
        in_specs=[pl.BlockSpec(memory_space=pltpu.SMEM)] * smem
        + [pl.BlockSpec(memory_space=pltpu.VMEM)] * (len(args) - smem),
        out_specs=[pl.BlockSpec(memory_space=pltpu.VMEM)] * len(out_shapes),
        compiler_params=pltpu.CompilerParams(vmem_limit_bytes=VMEM_LIMIT),
        cost_estimate=FREE,
        name=name,
    )(*args)


def place_kernel(planes, summands, columns, aliased, table_ref, *refs):
    blocks = list(refs[: sum(summands)])
    out = refs[len(blocks) + aliased]
    *totals, sems = refs[len(blocks) + aliased + 1 :]
    row = device_row(planes)
    stores = []
    for total, terms, places in zip(totals, summands, columns):
        taken, blocks = blocks[:terms], blocks[terms:]
        if terms > 1:
            total[...] = taken[0][0 : total.shape[0], :] + taken[1][0 : total.shape[0], :]
        else:
            total = taken[0]
        width = total.shape[1] // len(places)
        for part, (where, offset) in enumerate(places):
            column = pl.multiple_of((table_ref[row, where] + offset) * 128, 128)
            stores.append(
                pltpu.make_async_copy(
                    total.at[:, pl.ds(part * width, width)], out.at[:, pl.ds(column, width)], sems.at[len(stores)]
                )
            )
            stores[-1].start()
    for store in stores:
        store.wait()


def place(table, planes, pieces, shape, into, name):
    blocks = [block for terms, _ in pieces for block in terms]
    columns = [places for _, places in pieces]
    aliased = 0 if into is None else 1
    near, far = pl.BlockSpec(memory_space=pltpu.VMEM), pl.BlockSpec(memory_space=pl.ANY)
    return pl.pallas_call(
        functools.partial(place_kernel, planes, [len(terms) for terms, _ in pieces], columns, aliased),
        out_shape=jax.ShapeDtypeStruct(shape, jnp.float32),
        in_specs=[pl.BlockSpec(memory_space=pltpu.SMEM)] + [near] * len(blocks) + [far] * aliased,
        out_specs=far,
        scratch_shapes=[pltpu.VMEM((shape[0], terms[0].shape[1]), jnp.float32) for terms, _ in pieces]
        + [pltpu.SemaphoreType.DMA((sum(map(len, columns)),))],
        input_output_aliases={1 + len(blocks): 0} if aliased else {},
        compiler_params=pltpu.CompilerParams(vmem_limit_bytes=VMEM_LIMIT),
        cost_estimate=FREE,
        name=name,
    )(table, *blocks, *([into] if aliased else []))


def column_table(levels, planes, block):
    per_plane = levels // planes
    table = np.zeros((levels * 4 * planes, 16), np.int32)

    def column(level, side, core):
        return ((level % per_plane * 2 + side) * 2 + core) * block

    for z in range(levels):
        for x in range(2):
            for c in range(2):
                for y in range(planes):
                    row = [int(z // per_plane == y)]
                    for step in (-1, 1):
                        for core in range(2):
                            level = (z + step * (1 - 2 * core)) % levels
                            if level // per_plane == y:
                                row += [column(level, x, core), column(level, 1 - x, core)]
                    level = z if row[0] else (z + levels // 2) % levels
                    for core in (c, 1 - c):
                        row += [column(level, x, core), column(level, 1 - x, core)]
                    table[((z * 2 + x) * 2 + c) * planes + y, : len(row)] = row
    return table


def ringed(log_derivs, coefficients):
    rows, params = log_derivs.shape
    samples = rows * lax.axis_size("smp")
    levels, planes = lax.axis_size("smp") // 4, lax.axis_size("par")
    per_plane = levels // planes
    shape = (rows, rows * 4 * per_plane)
    scale = 1.0 / samples

    def moves(to):
        pairs = []
        for z in range(levels):
            for x in range(2):
                for c in range(2):
                    for y in range(planes):
                        tz, tx, tc, ty = to(z, x, c, y)
                        target = ((tz % levels) * 2 + tx) * 2 + tc
                        pairs.append((((z * 2 + x) * 2 + c) * planes + y, target * planes + ty))
        return pairs

    def holder(z):
        return z % levels // per_plane

    ring = moves(lambda z, x, c, y: (z + 1 - 2 * c, x, c, y))
    over_core = moves(lambda z, x, c, y: (z, x, 1 - c, y))
    over_side = moves(lambda z, x, c, y: (z, 1 - x, c, y))
    over_plane = moves(lambda z, x, c, y: (z, x, c, 1 - y))
    diagonal = moves(lambda z, x, c, y: (z, 1 - x, c, 1 - y))
    turns = [moves(lambda z, x, c, y, k=k: (z + k, x, c, y)) for k in range(1, levels)]

    def to_holder(step, side, swap):
        return moves(lambda z, x, c, y: (z, x ^ side, c ^ y ^ swap, holder(z - step * (1 - 2 * c))))

    def send(value, pairs):
        return lax.ppermute(value, BOTH, pairs)

    table = jnp.asarray(column_table(levels, planes, rows // 128))

    core_rows = send(log_derivs, over_core)
    one = send(log_derivs, ring)

    side_rows = send(log_derivs, over_side)

    coefficients = coefficients[None, :]
    stats = block_stats(log_derivs, core_rows, coefficients, send(coefficients, over_core))
    stats = merge(stats, *[send(stats, turn) for turn in turns])
    one, side_rows = lax.optimization_barrier((one, side_rows, stats))[:2]
    two = send(one, ring)
    stats = merge(stats, send(stats, over_side))
    side_core_rows = send(side_rows, over_core)
    all_rows = (log_derivs, core_rows, side_rows, side_core_rows)

    def one_level(block, step, name):
        out = kernel_call(functools.partial(one_level_kernel, scale), [(rows, rows)] * 4, name, stats, *all_rows, block)
        sent = [[send(out[2 * k + swap], to_holder(step, 1 - k, swap)) for swap in range(2)] for k in range(2)]
        return out, sent[::-1]

    out, near = one_level(one, 1, "products_near")
    share = params // lax.axis_size("smp")

    own_level = kernel_call(
        functools.partial(own_level_kernel, scale),
        [(2 * rows, rows)] * 2,
        "products_level",
        stats,
        *all_rows,
        after(log_derivs, out[0]),
    )
    two = after(two, *near[1], *near[0], *own_level)
    three = send(two, ring)
    keep_own, keep_side, sent_own, sent_side = kernel_call(
        functools.partial(across_level_kernel, scale, planes, 0),
        [(2 * rows, rows)] * 4,
        "products_across",
        table,
        stats,
        *all_rows,
        two,
        *own_level,
        smem=1,
    )
    got_own = send(sent_own, over_plane)
    got_side = send(sent_side, diagonal)
    from_side = send(keep_side, over_side)

    out, far = one_level(three, -1, "products_far")

    got_own = after(got_own, out[0])
    own, side = kernel_call(across_kernel, [(rows, rows)] * 2, "sum_across", keep_own, got_own, from_side, got_side)
    across_own, across_side = send(own, over_core), send(side, over_core)
    update = lax.dynamic_slice(after(stats, out[0]), (1, lax.axis_index("smp") * share), (1, share))[0]
    update = update / jnp.sqrt(jnp.float32(samples))
    gram = place(
        table,
        planes,
        [(near[0], [(1, 0)]), (near[1], [(2, 0)]), ((keep_own, got_own), [(5, 0)]), ((from_side, got_side), [(6, 0)])],
        shape,
        None,
        "place_most",
    )
    gram = after(gram, *far[1], *far[0])
    gram = place(
        table,
        planes,
        [(far[1], [(4, 0)]), (far[0], [(3, 0)]), ((across_own,), [(7, 0)]), ((across_side,), [(8, 0)])],
        shape,
        gram,
        "place_last",
    )
    return (gram, update)


def solution(mesh):
    placed = (P("smp", "par"), P("smp"))
    levels, planes = mesh.shape["smp"] // 4, mesh.shape["par"]
    return jax.shard_map(
        ringed if planes == 2 and levels == 2 * planes else gathered,
        mesh=mesh,
        in_specs=placed,
        out_specs=(P("smp", "par"), P(("par", "smp"))),
        check_vma=False,
    )
```

```python
import functools

import jax
import jax.numpy as jnp
import numpy as np
from jax import lax
from jax.experimental import pallas as pl
from jax.experimental.pallas import tpu as pltpu
from jax.sharding import PartitionSpec as P

BOTH = ("smp", "par")
VMEM_LIMIT = 16 * 1024 * 1024
LONG = pl.CostEstimate(flops=4_000_000_000, bytes_accessed=0, transcendentals=0)
FREE = pl.CostEstimate(flops=0, bytes_accessed=0, transcendentals=0)


def row_products(left_rows, right_rows):
    return lax.dot_general(
        left_rows,
        right_rows,
        (((1,), (1,)), ((), ())),
        precision=lax.Precision.HIGHEST,
        preferred_element_type=jnp.float32,
    )


def gathered(log_derivs, coefficients):
    samples = log_derivs.shape[0] * lax.axis_size("smp")
    column_total = lax.psum(jnp.sum(log_derivs, axis=0), "smp")
    centred = (log_derivs - column_total[None, :] / samples) / jnp.sqrt(jnp.float32(samples))
    partial_gram = row_products(centred, lax.all_gather(centred, "smp", axis=0, tiled=True))
    gram = lax.psum_scatter(partial_gram, "par", scatter_dimension=1, tiled=True)
    update_term = lax.dot_general(
        coefficients,
        centred,
        (((0,), (0,)), ((), ())),
        precision=lax.Precision.HIGHEST,
        preferred_element_type=jnp.float32,
    )
    update = lax.psum_scatter(update_term, "smp", scatter_dimension=0, tiled=True)
    return (gram, update)


def after(value, *others):
    return lax.optimization_barrier((value, *others))[0]


def stats_kernel(rows_ref, other_ref, coef_ref, other_coef_ref, stats_ref):
    blocks = (rows_ref, other_ref)
    mean = sum(jnp.sum(ref[...], axis=0, keepdims=True) for ref in blocks) / sum(ref.shape[0] for ref in blocks)
    stats_ref[...] = jnp.zeros_like(stats_ref)
    stats_ref[0:1, :] = mean
    stats_ref[1:2, :] = sum(
        jnp.dot(coef[...], ref[...] - mean, precision=lax.Precision.HIGHEST, preferred_element_type=jnp.float32)
        for coef, ref in zip((coef_ref, other_coef_ref), blocks)
    )
    total = sum(jnp.sum(coef[...], axis=1, keepdims=True) for coef in (coef_ref, other_coef_ref))
    stats_ref[2:3, :] = jnp.broadcast_to(total, mean.shape)


def block_stats(rows, other, coefficients, other_coefficients):
    return kernel_call(
        stats_kernel, [(8, rows.shape[1])], "block_stats", rows, other, coefficients, other_coefficients
    )[0]


def merge_kernel(count, *refs):
    parts, out = refs[:count], refs[count]
    mean = sum(p[0:1, :] for p in parts) / count
    out[...] = jnp.zeros_like(out)
    out[0:1, :] = mean
    out[1:2, :] = sum(p[1:2, :] + p[2:3, :] * (p[0:1, :] - mean) for p in parts)
    out[2:3, :] = sum(p[2:3, :] for p in parts)


def merge(*parts):
    return kernel_call(functools.partial(merge_kernel, len(parts)), [parts[0].shape], "merge", *parts)[0]


def split(values):
    high = values.astype(jnp.bfloat16)
    return high, (values - high.astype(jnp.float32)).astype(jnp.bfloat16)


def dot_nt(left, right):
    return lax.dot_general(left, right, (((1,), (1,)), ((), ())), preferred_element_type=jnp.float32)


def device_row(planes):
    return lax.axis_index("smp") * planes + lax.axis_index("par")


def product_of(row_ref, mean, high, low, scale):
    row_high, row_low = split(row_ref[...] - mean)
    return (dot_nt(row_high, high) + (dot_nt(row_high, low) + dot_nt(row_low, high))) * scale


def one_level_kernel(scale, mean_ref, *refs):
    rows, block, outs = refs[:4], refs[4], refs[5:]
    mean = mean_ref[0:1, :]
    high, low = split(block[...] - mean)
    straight = lax.axis_index("par") == 0
    for k, side in enumerate((1, 0)):
        same = product_of(rows[2 * side], mean, high, low, scale)
        other = product_of(rows[2 * side + 1], mean, high, low, scale)
        outs[2 * k][...] = jnp.where(straight, same, other)
        outs[2 * k + 1][...] = jnp.where(straight, other, same)


def own_level_kernel(scale, mean_ref, *refs):
    rows, block, outs = refs[:4], refs[4], refs[5:]
    mean = mean_ref[0:1, :]
    high, low = split(block[...] - mean)
    height = rows[0].shape[0]
    for k, row in enumerate(rows):
        outs[k // 2][k % 2 * height : (k % 2 + 1) * height, :] = product_of(row, mean, high, low, scale)


def across_level_kernel(scale, planes, flag_at, table_ref, mean_ref, *refs):
    rows, block, level, outs = refs[:4], refs[4], refs[5:7], refs[7:]
    mean = mean_ref[0:1, :]
    first = table_ref[device_row(planes), flag_at] == 1
    high, low = split(block[...] - mean)
    height = rows[0].shape[0]
    for k, row in enumerate(rows):
        total = product_of(row, mean, high, low, scale)
        place = slice(k % 2 * height, (k % 2 + 1) * height)
        here = level[k // 2][place, :]
        outs[k // 2][place, :] = jnp.where(first, here, total)
        outs[2 + k // 2][place, :] = jnp.where(first, total, here)


def across_kernel(keep_own, got_own, from_side, got_side, own, side):
    height = own.shape[0]
    own[...] = keep_own[height:, :] + got_own[height:, :]
    side[...] = from_side[height:, :] + got_side[height:, :]


def kernel_call(kernel, out_shapes, name, *args, smem=0, cost=FREE):
    return pl.pallas_call(
        kernel,
        out_shape=[jax.ShapeDtypeStruct(s, jnp.float32) for s in out_shapes],
        in_specs=[pl.BlockSpec(memory_space=pltpu.SMEM)] * smem
        + [pl.BlockSpec(memory_space=pltpu.VMEM)] * (len(args) - smem),
        out_specs=[pl.BlockSpec(memory_space=pltpu.VMEM)] * len(out_shapes),
        compiler_params=pltpu.CompilerParams(vmem_limit_bytes=VMEM_LIMIT),
        cost_estimate=cost,
        name=name,
    )(*args)


def place_kernel(planes, summands, columns, aliased, table_ref, *refs):
    blocks = list(refs[: sum(summands)])
    out = refs[len(blocks) + aliased]
    *totals, sems = refs[len(blocks) + aliased + 1 :]
    row = device_row(planes)
    stores = []
    for total, terms, places in zip(totals, summands, columns):
        taken, blocks = blocks[:terms], blocks[terms:]
        if terms > 1:
            total[...] = taken[0][0 : total.shape[0], :] + taken[1][0 : total.shape[0], :]
        else:
            total = taken[0]
        width = total.shape[1] // len(places)
        for part, (where, offset) in enumerate(places):
            column = pl.multiple_of((table_ref[row, where] + offset) * 128, 128)
            stores.append(
                pltpu.make_async_copy(
                    total.at[:, pl.ds(part * width, width)], out.at[:, pl.ds(column, width)], sems.at[len(stores)]
                )
            )
            stores[-1].start()
    for store in stores:
        store.wait()


def place(table, planes, pieces, shape, into, name):
    blocks = [block for terms, _ in pieces for block in terms]
    columns = [places for _, places in pieces]
    aliased = 0 if into is None else 1
    near, far = pl.BlockSpec(memory_space=pltpu.VMEM), pl.BlockSpec(memory_space=pl.ANY)
    return pl.pallas_call(
        functools.partial(place_kernel, planes, [len(terms) for terms, _ in pieces], columns, aliased),
        out_shape=jax.ShapeDtypeStruct(shape, jnp.float32),
        in_specs=[pl.BlockSpec(memory_space=pltpu.SMEM)] + [near] * len(blocks) + [far] * aliased,
        out_specs=far,
        scratch_shapes=[pltpu.VMEM((shape[0], terms[0].shape[1]), jnp.float32) for terms, _ in pieces]
        + [pltpu.SemaphoreType.DMA((sum(map(len, columns)),))],
        input_output_aliases={1 + len(blocks): 0} if aliased else {},
        compiler_params=pltpu.CompilerParams(vmem_limit_bytes=VMEM_LIMIT),
        cost_estimate=FREE,
        name=name,
    )(table, *blocks, *([into] if aliased else []))


def column_table(levels, planes, block):
    per_plane = levels // planes
    table = np.zeros((levels * 4 * planes, 16), np.int32)

    def column(level, side, core):
        return ((level % per_plane * 2 + side) * 2 + core) * block

    for z in range(levels):
        for x in range(2):
            for c in range(2):
                for y in range(planes):
                    row = [int(z // per_plane == y)]
                    for step in (-1, 1):
                        for core in range(2):
                            level = (z + step * (1 - 2 * core)) % levels
                            if level // per_plane == y:
                                row += [column(level, x, core), column(level, 1 - x, core)]
                    level = z if row[0] else (z + levels // 2) % levels
                    for core in (c, 1 - c):
                        row += [column(level, x, core), column(level, 1 - x, core)]
                    table[((z * 2 + x) * 2 + c) * planes + y, : len(row)] = row
    return table


def ringed(log_derivs, coefficients):
    rows, params = log_derivs.shape
    samples = rows * lax.axis_size("smp")
    levels, planes = lax.axis_size("smp") // 4, lax.axis_size("par")
    per_plane = levels // planes
    shape = (rows, rows * 4 * per_plane)
    scale = 1.0 / samples

    def moves(to):
        pairs = []
        for z in range(levels):
            for x in range(2):
                for c in range(2):
                    for y in range(planes):
                        tz, tx, tc, ty = to(z, x, c, y)
                        target = ((tz % levels) * 2 + tx) * 2 + tc
                        pairs.append((((z * 2 + x) * 2 + c) * planes + y, target * planes + ty))
        return pairs

    def holder(z):
        return z % levels // per_plane

    ring = moves(lambda z, x, c, y: (z + 1 - 2 * c, x, c, y))
    back = moves(lambda z, x, c, y: (z - 1 + 2 * c, x, c, y))
    over_core = moves(lambda z, x, c, y: (z, x, 1 - c, y))
    over_side = moves(lambda z, x, c, y: (z, 1 - x, c, y))
    over_plane = moves(lambda z, x, c, y: (z, x, c, 1 - y))
    diagonal = moves(lambda z, x, c, y: (z, 1 - x, c, 1 - y))
    turns = [moves(lambda z, x, c, y, k=k: (z + k, x, c, y)) for k in range(1, levels)]

    def to_holder(step, side, swap):
        return moves(lambda z, x, c, y: (z, x ^ side, c ^ y ^ swap, holder(z - step * (1 - 2 * c))))

    def send(value, pairs):
        return lax.ppermute(value, BOTH, pairs)

    table = jnp.asarray(column_table(levels, planes, rows // 128))

    core_rows = send(log_derivs, over_core)
    one = send(log_derivs, ring)

    side_rows = send(log_derivs, over_side)

    coefficients = coefficients[None, :]
    stats = block_stats(log_derivs, core_rows, coefficients, send(coefficients, over_core))
    stats = merge(stats, *[send(stats, turn) for turn in turns])
    one, side_rows = lax.optimization_barrier((one, side_rows, stats))[:2]
    two = send(one, ring)
    stats = merge(stats, send(stats, over_side))
    side_core_rows = send(side_rows, over_core)
    all_rows = (log_derivs, core_rows, side_rows, side_core_rows)

    def one_level(block, step, name):
        out = kernel_call(functools.partial(one_level_kernel, scale), [(rows, rows)] * 4, name, stats, *all_rows, block)
        sent = [[send(out[2 * k + swap], to_holder(step, 1 - k, swap)) for swap in range(2)] for k in range(2)]
        return out, sent[::-1]

    out, near = one_level(one, 1, "products_near")
    share = params // lax.axis_size("smp")

    own_level = kernel_call(
        functools.partial(own_level_kernel, scale),
        [(2 * rows, rows)] * 2,
        "products_level",
        stats,
        *all_rows,
        after(log_derivs, out[0]),
    )
    three = send(after(log_derivs, *near[1], *near[0], *own_level), back)
    two = after(two, *near[1], *near[0], *own_level)
    keep_own, keep_side, sent_own, sent_side = kernel_call(
        functools.partial(across_level_kernel, scale, planes, 0),
        [(2 * rows, rows)] * 4,
        "products_across",
        table,
        stats,
        *all_rows,
        two,
        *own_level,
        smem=1,
        cost=LONG,
    )
    got_own = send(sent_own, over_plane)
    got_side = send(sent_side, diagonal)
    from_side = send(keep_side, over_side)

    out, far = one_level(three, -1, "products_far")

    got_own = after(got_own, out[0])
    own, side = kernel_call(across_kernel, [(rows, rows)] * 2, "sum_across", keep_own, got_own, from_side, got_side)
    across_own, across_side = send(own, over_core), send(side, over_core)
    update = lax.dynamic_slice(after(stats, out[0]), (1, lax.axis_index("smp") * share), (1, share))[0]
    update = update / jnp.sqrt(jnp.float32(samples))
    gram = place(
        table,
        planes,
        [(near[0], [(1, 0)]), (near[1], [(2, 0)]), ((keep_own, got_own), [(5, 0)]), ((from_side, got_side), [(6, 0)])],
        shape,
        None,
        "place_most",
    )
    gram = after(gram, *far[1], *far[0])
    gram = place(
        table,
        planes,
        [(far[1], [(4, 0)]), (far[0], [(3, 0)]), ((across_own,), [(7, 0)]), ((across_side,), [(8, 0)])],
        shape,
        gram,
        "place_last",
    )
    return (gram, update)


def solution(mesh):
    placed = (P("smp", "par"), P("smp"))
    levels, planes = mesh.shape["smp"] // 4, mesh.shape["par"]
    return jax.shard_map(
        ringed if planes == 2 and levels == 2 * planes else gathered,
        mesh=mesh,
        in_specs=placed,
        out_specs=(P("smp", "par"), P(("par", "smp"))),
        check_vma=False,
    )
```

```python
import functools

import jax
import jax.numpy as jnp
import numpy as np
from jax import lax
from jax.experimental import pallas as pl
from jax.experimental.pallas import tpu as pltpu
from jax.sharding import PartitionSpec as P

BOTH = ("smp", "par")
VMEM_LIMIT = 16 * 1024 * 1024
LONG = pl.CostEstimate(flops=4_000_000_000, bytes_accessed=0, transcendentals=0)
FREE = pl.CostEstimate(flops=0, bytes_accessed=0, transcendentals=0)


def row_products(left_rows, right_rows):
    return lax.dot_general(
        left_rows,
        right_rows,
        (((1,), (1,)), ((), ())),
        precision=lax.Precision.HIGHEST,
        preferred_element_type=jnp.float32,
    )


def gathered(log_derivs, coefficients):
    samples = log_derivs.shape[0] * lax.axis_size("smp")
    column_total = lax.psum(jnp.sum(log_derivs, axis=0), "smp")
    centred = (log_derivs - column_total[None, :] / samples) / jnp.sqrt(jnp.float32(samples))
    partial_gram = row_products(centred, lax.all_gather(centred, "smp", axis=0, tiled=True))
    gram = lax.psum_scatter(partial_gram, "par", scatter_dimension=1, tiled=True)
    update_term = lax.dot_general(
        coefficients,
        centred,
        (((0,), (0,)), ((), ())),
        precision=lax.Precision.HIGHEST,
        preferred_element_type=jnp.float32,
    )
    update = lax.psum_scatter(update_term, "smp", scatter_dimension=0, tiled=True)
    return (gram, update)


def after(value, *others):
    return lax.optimization_barrier((value, *others))[0]


def stats_kernel(rows_ref, other_ref, coef_ref, other_coef_ref, stats_ref):
    blocks = (rows_ref, other_ref)
    mean = sum(jnp.sum(ref[...], axis=0, keepdims=True) for ref in blocks) / sum(ref.shape[0] for ref in blocks)
    stats_ref[...] = jnp.zeros_like(stats_ref)
    stats_ref[0:1, :] = mean
    stats_ref[1:2, :] = sum(
        jnp.dot(coef[...], ref[...] - mean, precision=lax.Precision.HIGHEST, preferred_element_type=jnp.float32)
        for coef, ref in zip((coef_ref, other_coef_ref), blocks)
    )
    total = sum(jnp.sum(coef[...], axis=1, keepdims=True) for coef in (coef_ref, other_coef_ref))
    stats_ref[2:3, :] = jnp.broadcast_to(total, mean.shape)


def block_stats(rows, other, coefficients, other_coefficients):
    return kernel_call(
        stats_kernel, [(8, rows.shape[1])], "block_stats", rows, other, coefficients, other_coefficients
    )[0]


def merge_kernel(count, *refs):
    parts, out = refs[:count], refs[count]
    mean = sum(p[0:1, :] for p in parts) / count
    out[...] = jnp.zeros_like(out)
    out[0:1, :] = mean
    out[1:2, :] = sum(p[1:2, :] + p[2:3, :] * (p[0:1, :] - mean) for p in parts)
    out[2:3, :] = sum(p[2:3, :] for p in parts)


def merge(*parts):
    return kernel_call(functools.partial(merge_kernel, len(parts)), [parts[0].shape], "merge", *parts)[0]


def split(values):
    high = values.astype(jnp.bfloat16)
    return high, (values - high.astype(jnp.float32)).astype(jnp.bfloat16)


def dot_nt(left, right):
    return lax.dot_general(left, right, (((1,), (1,)), ((), ())), preferred_element_type=jnp.float32)


def device_row(planes):
    return lax.axis_index("smp") * planes + lax.axis_index("par")


def product_of(row_ref, mean, high, low, scale):
    row_high, row_low = split(row_ref[...] - mean)
    return (dot_nt(row_high, high) + (dot_nt(row_high, low) + dot_nt(row_low, high))) * scale


def one_level_kernel(scale, mean_ref, *refs):
    rows, block, outs = refs[:4], refs[4], refs[5:]
    mean = mean_ref[0:1, :]
    high, low = split(block[...] - mean)
    straight = lax.axis_index("par") == 0
    for k, side in enumerate((1, 0)):
        same = product_of(rows[2 * side], mean, high, low, scale)
        other = product_of(rows[2 * side + 1], mean, high, low, scale)
        outs[2 * k][...] = jnp.where(straight, same, other)
        outs[2 * k + 1][...] = jnp.where(straight, other, same)


def own_level_kernel(scale, mean_ref, *refs):
    rows, block, outs = refs[:4], refs[4], refs[5:]
    mean = mean_ref[0:1, :]
    high, low = split(block[...] - mean)
    height = rows[0].shape[0]
    for k, row in enumerate(rows):
        outs[k // 2][k % 2 * height : (k % 2 + 1) * height, :] = product_of(row, mean, high, low, scale)


def across_level_kernel(scale, planes, flag_at, table_ref, mean_ref, *refs):
    rows, block, level, outs = refs[:4], refs[4], refs[5:7], refs[7:]
    mean = mean_ref[0:1, :]
    first = table_ref[device_row(planes), flag_at] == 1
    high, low = split(block[...] - mean)
    height = rows[0].shape[0]
    for k, row in enumerate(rows):
        total = product_of(row, mean, high, low, scale)
        place = slice(k % 2 * height, (k % 2 + 1) * height)
        here = level[k // 2][place, :]
        outs[k // 2][place, :] = jnp.where(first, here, total)
        outs[2 + k // 2][place, :] = jnp.where(first, total, here)


def across_kernel(keep_own, got_own, from_side, got_side, own, side):
    height = own.shape[0]
    own[...] = keep_own[height:, :] + got_own[height:, :]
    side[...] = from_side[height:, :] + got_side[height:, :]


def kernel_call(kernel, out_shapes, name, *args, smem=0, cost=FREE):
    return pl.pallas_call(
        kernel,
        out_shape=[jax.ShapeDtypeStruct(s, jnp.float32) for s in out_shapes],
        in_specs=[pl.BlockSpec(memory_space=pltpu.SMEM)] * smem
        + [pl.BlockSpec(memory_space=pltpu.VMEM)] * (len(args) - smem),
        out_specs=[pl.BlockSpec(memory_space=pltpu.VMEM)] * len(out_shapes),
        compiler_params=pltpu.CompilerParams(vmem_limit_bytes=VMEM_LIMIT),
        cost_estimate=cost,
        name=name,
    )(*args)


def place_kernel(planes, summands, columns, aliased, table_ref, *refs):
    blocks = list(refs[: sum(summands)])
    out = refs[len(blocks) + aliased]
    *totals, sems = refs[len(blocks) + aliased + 1 :]
    row = device_row(planes)
    stores = []
    for total, terms, places in zip(totals, summands, columns):
        taken, blocks = blocks[:terms], blocks[terms:]
        if terms > 1:
            total[...] = taken[0][0 : total.shape[0], :] + taken[1][0 : total.shape[0], :]
        else:
            total = taken[0]
        width = total.shape[1] // len(places)
        for part, (where, offset) in enumerate(places):
            column = pl.multiple_of((table_ref[row, where] + offset) * 128, 128)
            stores.append(
                pltpu.make_async_copy(
                    total.at[:, pl.ds(part * width, width)], out.at[:, pl.ds(column, width)], sems.at[len(stores)]
                )
            )
            stores[-1].start()
    for store in stores:
        store.wait()


def place(table, planes, pieces, shape, into, name):
    blocks = [block for terms, _ in pieces for block in terms]
    columns = [places for _, places in pieces]
    aliased = 0 if into is None else 1
    near, far = pl.BlockSpec(memory_space=pltpu.VMEM), pl.BlockSpec(memory_space=pl.ANY)
    return pl.pallas_call(
        functools.partial(place_kernel, planes, [len(terms) for terms, _ in pieces], columns, aliased),
        out_shape=jax.ShapeDtypeStruct(shape, jnp.float32),
        in_specs=[pl.BlockSpec(memory_space=pltpu.SMEM)] + [near] * len(blocks) + [far] * aliased,
        out_specs=far,
        scratch_shapes=[pltpu.VMEM((shape[0], terms[0].shape[1]), jnp.float32) for terms, _ in pieces]
        + [pltpu.SemaphoreType.DMA((sum(map(len, columns)),))],
        input_output_aliases={1 + len(blocks): 0} if aliased else {},
        compiler_params=pltpu.CompilerParams(vmem_limit_bytes=VMEM_LIMIT),
        cost_estimate=FREE,
        name=name,
    )(table, *blocks, *([into] if aliased else []))


def column_table(levels, planes, block):
    per_plane = levels // planes
    table = np.zeros((levels * 4 * planes, 16), np.int32)

    def column(level, side, core):
        return ((level % per_plane * 2 + side) * 2 + core) * block

    for z in range(levels):
        for x in range(2):
            for c in range(2):
                for y in range(planes):
                    row = [int(z // per_plane == y)]
                    for step in (-1, 1):
                        for core in range(2):
                            level = (z + step * (1 - 2 * core)) % levels
                            if level // per_plane == y:
                                row += [column(level, x, core), column(level, 1 - x, core)]
                    level = z if row[0] else (z + levels // 2) % levels
                    for core in (c, 1 - c):
                        row += [column(level, x, core), column(level, 1 - x, core)]
                    table[((z * 2 + x) * 2 + c) * planes + y, : len(row)] = row
    return table


def ringed(log_derivs, coefficients):
    rows, params = log_derivs.shape
    samples = rows * lax.axis_size("smp")
    levels, planes = lax.axis_size("smp") // 4, lax.axis_size("par")
    per_plane = levels // planes
    shape = (rows, rows * 4 * per_plane)
    scale = 1.0 / samples

    def moves(to):
        pairs = []
        for z in range(levels):
            for x in range(2):
                for c in range(2):
                    for y in range(planes):
                        tz, tx, tc, ty = to(z, x, c, y)
                        target = ((tz % levels) * 2 + tx) * 2 + tc
                        pairs.append((((z * 2 + x) * 2 + c) * planes + y, target * planes + ty))
        return pairs

    def holder(z):
        return z % levels // per_plane

    ring = moves(lambda z, x, c, y: (z + 1 - 2 * c, x, c, y))
    back = moves(lambda z, x, c, y: (z - 1 + 2 * c, x, c, y))
    over_core = moves(lambda z, x, c, y: (z, x, 1 - c, y))
    over_side = moves(lambda z, x, c, y: (z, 1 - x, c, y))
    over_plane = moves(lambda z, x, c, y: (z, x, c, 1 - y))
    diagonal = moves(lambda z, x, c, y: (z, 1 - x, c, 1 - y))
    turns = [moves(lambda z, x, c, y, k=k: (z + k, x, c, y)) for k in range(1, levels)]

    def to_holder(step, side, swap):
        return moves(lambda z, x, c, y: (z, x ^ side, c ^ y ^ swap, holder(z - step * (1 - 2 * c))))

    def send(value, pairs):
        return lax.ppermute(value, BOTH, pairs)

    table = jnp.asarray(column_table(levels, planes, rows // 128))

    core_rows = send(log_derivs, over_core)
    one = send(log_derivs, ring)


    coefficients = coefficients[None, :]
    other_coefficients = send(coefficients, over_core)
    side_rows = send(after(log_derivs, other_coefficients), over_side)
    stats = block_stats(log_derivs, core_rows, coefficients, other_coefficients)
    stats = merge(stats, *[send(stats, turn) for turn in turns])
    one, side_rows = lax.optimization_barrier((one, side_rows, stats))[:2]
    two = send(one, ring)
    stats = merge(stats, send(stats, over_side))
    side_core_rows = send(side_rows, over_core)
    all_rows = (log_derivs, core_rows, side_rows, side_core_rows)

    def one_level(block, step, name):
        out = kernel_call(functools.partial(one_level_kernel, scale), [(rows, rows)] * 4, name, stats, *all_rows, block)
        sent = [[send(out[2 * k + swap], to_holder(step, 1 - k, swap)) for swap in range(2)] for k in range(2)]
        return out, sent[::-1]

    out, near = one_level(one, 1, "products_near")
    share = params // lax.axis_size("smp")

    own_level = kernel_call(
        functools.partial(own_level_kernel, scale),
        [(2 * rows, rows)] * 2,
        "products_level",
        stats,
        *all_rows,
        after(log_derivs, out[0]),
    )
    near = [after(piece, *near[1]) for piece in near[0]], near[1]
    three = send(after(log_derivs, *near[1], *near[0], *own_level), back)
    two = after(two, *near[1], *near[0], *own_level)
    keep_own, keep_side, sent_own, sent_side = kernel_call(
        functools.partial(across_level_kernel, scale, planes, 0),
        [(2 * rows, rows)] * 4,
        "products_across",
        table,
        stats,
        *all_rows,
        two,
        *own_level,
        smem=1,
        cost=LONG,
    )
    got_own = send(sent_own, over_plane)
    got_side = send(sent_side, diagonal)
    from_side = send(keep_side, over_side)

    out, far = one_level(three, -1, "products_far")

    got_own = after(got_own, out[0])
    own, side = kernel_call(across_kernel, [(rows, rows)] * 2, "sum_across", keep_own, got_own, from_side, got_side)
    across_own, across_side = send(own, over_core), send(side, over_core)
    update = lax.dynamic_slice(after(stats, out[0]), (1, lax.axis_index("smp") * share), (1, share))[0]
    update = update / jnp.sqrt(jnp.float32(samples))
    gram = place(
        table,
        planes,
        [(near[0], [(1, 0)]), (near[1], [(2, 0)]), ((keep_own, got_own), [(5, 0)]), ((from_side, got_side), [(6, 0)])],
        shape,
        None,
        "place_most",
    )
    gram = after(gram, *far[1], *far[0])
    gram = place(
        table,
        planes,
        [(far[1], [(4, 0)]), (far[0], [(3, 0)]), ((across_own,), [(7, 0)]), ((across_side,), [(8, 0)])],
        shape,
        gram,
        "place_last",
    )
    return (gram, update)


def solution(mesh):
    placed = (P("smp", "par"), P("smp"))
    levels, planes = mesh.shape["smp"] // 4, mesh.shape["par"]
    return jax.shard_map(
        ringed if planes == 2 and levels == 2 * planes else gathered,
        mesh=mesh,
        in_specs=placed,
        out_specs=(P("smp", "par"), P(("par", "smp"))),
        check_vma=False,
    )
```

```python
import functools

import jax
import jax.numpy as jnp
from jax import lax
from jax.experimental import pallas as pl
from jax.experimental.pallas import tpu as pltpu
from jax.sharding import PartitionSpec as P

BOTH = ("smp", "par")
VMEM_LIMIT = 16 * 1024 * 1024
LONG = pl.CostEstimate(flops=4_000_000_000, bytes_accessed=0, transcendentals=0)
FREE = pl.CostEstimate(flops=0, bytes_accessed=0, transcendentals=0)


def row_products(left_rows, right_rows):
    return lax.dot_general(
        left_rows,
        right_rows,
        (((1,), (1,)), ((), ())),
        precision=lax.Precision.HIGHEST,
        preferred_element_type=jnp.float32,
    )


def gathered(log_derivs, coefficients):
    samples = log_derivs.shape[0] * lax.axis_size("smp")
    column_total = lax.psum(jnp.sum(log_derivs, axis=0), "smp")
    centred = (log_derivs - column_total[None, :] / samples) / jnp.sqrt(jnp.float32(samples))
    partial_gram = row_products(centred, lax.all_gather(centred, "smp", axis=0, tiled=True))
    gram = lax.psum_scatter(partial_gram, "par", scatter_dimension=1, tiled=True)
    update_term = lax.dot_general(
        coefficients,
        centred,
        (((0,), (0,)), ((), ())),
        precision=lax.Precision.HIGHEST,
        preferred_element_type=jnp.float32,
    )
    update = lax.psum_scatter(update_term, "smp", scatter_dimension=0, tiled=True)
    return (gram, update)


def after(value, *others):
    return lax.optimization_barrier((value, *others))[0]


def stats_kernel(rows_ref, other_ref, coef_ref, other_coef_ref, stats_ref):
    blocks = (rows_ref, other_ref)
    mean = sum(jnp.sum(ref[...], axis=0, keepdims=True) for ref in blocks) / sum(ref.shape[0] for ref in blocks)
    stats_ref[...] = jnp.zeros_like(stats_ref)
    stats_ref[0:1, :] = mean
    stats_ref[1:2, :] = sum(
        jnp.dot(coef[...], ref[...] - mean, precision=lax.Precision.HIGHEST, preferred_element_type=jnp.float32)
        for coef, ref in zip((coef_ref, other_coef_ref), blocks)
    )
    total = sum(jnp.sum(coef[...], axis=1, keepdims=True) for coef in (coef_ref, other_coef_ref))
    stats_ref[2:3, :] = jnp.broadcast_to(total, mean.shape)


def block_stats(rows, other, coefficients, other_coefficients):
    return kernel_call(
        stats_kernel, [(8, rows.shape[1])], "block_stats", rows, other, coefficients, other_coefficients
    )[0]


def merge_kernel(count, *refs):
    parts, out = refs[:count], refs[count]
    mean = sum(p[0:1, :] for p in parts) / count
    out[...] = jnp.zeros_like(out)
    out[0:1, :] = mean
    out[1:2, :] = sum(p[1:2, :] + p[2:3, :] * (p[0:1, :] - mean) for p in parts)
    out[2:3, :] = sum(p[2:3, :] for p in parts)


def merge(*parts):
    return kernel_call(functools.partial(merge_kernel, len(parts)), [parts[0].shape], "merge", *parts)[0]


def split(values):
    high = values.astype(jnp.bfloat16)
    return high, (values - high.astype(jnp.float32)).astype(jnp.bfloat16)


def dot_nt(left, right):
    return lax.dot_general(left, right, (((1,), (1,)), ((), ())), preferred_element_type=jnp.float32)


def entry(dims, which):
    levels, planes, block = dims
    per_plane = levels // planes
    here, plane = lax.axis_index("smp"), lax.axis_index("par")
    level, side, core = lax.div(here, 4), lax.rem(lax.div(here, 2), 2), lax.rem(here, 2)

    def off(step, core):
        return lax.rem(level - step * (1 - 2 * core) + levels, levels)

    def held(z):
        return lax.div(z, per_plane) == plane

    if which == 0:
        return held(level)
    if which >= 9:
        return held(off(1 if which == 9 else -1, core))
    if which <= 4:
        step = 1 if which <= 2 else -1
        first = held(off(step, 0))
        z, of_core = jnp.where(first, off(step, 0), off(step, 1)), jnp.where(first, 0, 1)
    else:
        z = jnp.where(held(level), level, lax.rem(level + levels // 2, levels))
        of_core = core if which <= 6 else 1 - core
    of_side = side if which % 2 == 1 else 1 - side
    return ((lax.rem(z, per_plane) * 2 + of_side) * 2 + of_core) * block


def product_of(row_ref, mean, high, low, scale):
    row_high, row_low = split(row_ref[...] - mean)
    return (dot_nt(row_high, high) + (dot_nt(row_high, low) + dot_nt(row_low, high))) * scale


def one_level_kernel(scale, dims, flag_at, mean_ref, *refs):
    rows, block, outs = refs[:4], refs[4], refs[5:]
    mean = mean_ref[0:1, :]
    high, low = split(block[...] - mean)
    straight = entry(dims, flag_at)
    for k, side in enumerate((1, 0)):
        same = product_of(rows[2 * side], mean, high, low, scale)
        other = product_of(rows[2 * side + 1], mean, high, low, scale)
        outs[2 * k][...] = jnp.where(straight, same, other)
        outs[2 * k + 1][...] = jnp.where(straight, other, same)


def own_level_kernel(scale, mean_ref, *refs):
    rows, block, outs = refs[:4], refs[4], refs[5:]
    mean = mean_ref[0:1, :]
    high, low = split(block[...] - mean)
    height = rows[0].shape[0]
    for k, row in enumerate(rows):
        outs[k // 2][k % 2 * height : (k % 2 + 1) * height, :] = product_of(row, mean, high, low, scale)


def across_level_kernel(scale, dims, mean_ref, *refs):
    rows, block, level, outs = refs[:4], refs[4], refs[5:7], refs[7:]
    mean = mean_ref[0:1, :]
    first = entry(dims, 0)
    high, low = split(block[...] - mean)
    height = rows[0].shape[0]
    for k, row in enumerate(rows):
        total = product_of(row, mean, high, low, scale)
        place = slice(k % 2 * height, (k % 2 + 1) * height)
        here = level[k // 2][place, :]
        outs[k // 2][place, :] = jnp.where(first, here, total)
        outs[2 + k // 2][place, :] = jnp.where(first, total, here)


def across_kernel(keep_own, got_own, from_side, got_side, own, side):
    height = own.shape[0]
    own[...] = keep_own[height:, :] + got_own[height:, :]
    side[...] = from_side[height:, :] + got_side[height:, :]


def kernel_call(kernel, out_shapes, name, *args, cost=FREE):
    return pl.pallas_call(
        kernel,
        out_shape=[jax.ShapeDtypeStruct(s, jnp.float32) for s in out_shapes],
        in_specs=[pl.BlockSpec(memory_space=pltpu.VMEM)] * len(args),
        out_specs=[pl.BlockSpec(memory_space=pltpu.VMEM)] * len(out_shapes),
        compiler_params=pltpu.CompilerParams(vmem_limit_bytes=VMEM_LIMIT),
        cost_estimate=cost,
        name=name,
    )(*args)


def place_kernel(dims, apart, summands, columns, aliased, *refs):
    blocks = list(refs[: sum(map(len, summands))])
    out = refs[len(blocks) + aliased]
    scratch = list(refs[len(blocks) + aliased + 1 :])
    sems = scratch.pop()
    if apart:
        loads = []
        for block in blocks:
            here = scratch.pop(0)
            loads.append(pltpu.make_async_copy(block.at[pl.ds(0, here.shape[0])], here, sems.at[len(loads)]))
            loads[-1].start()
        blocks = [load.dst_ref for load in loads]
        for load in loads:
            load.wait()
    copies = []
    for total, flags, places in zip(scratch, summands, columns):
        taken, blocks = blocks[: len(flags)], blocks[len(flags) :]
        value = 0.0
        for block, flag_at in zip(taken, flags):
            part = block[0 : total.shape[0], :]
            value += part if flag_at is None else jnp.where(entry(dims, flag_at), part, 0.0)
        total[...] = value
        width = total.shape[1] // len(places)
        for part, (where, offset) in enumerate(places):
            column = pl.multiple_of((entry(dims, where) + offset) * 128, 128)
            copy = pltpu.make_async_copy(
                total.at[:, pl.ds(part * width, width)],
                out.at[:, pl.ds(column, width)],
                sems.at[apart * sum(map(len, summands)) + len(copies)],
            )
            copy.start()
            copies.append(copy)
    for copy in copies:
        copy.wait()


def place(dims, pieces, shape, into, name, apart=False):
    pieces = [([t if isinstance(t, tuple) else (t, None) for t in terms], places) for terms, places in pieces]
    blocks = [block for terms, _ in pieces for block, _ in terms]
    columns = [places for _, places in pieces]
    aliased = 0 if into is None else 1
    near, far = pl.BlockSpec(memory_space=pltpu.VMEM), pl.BlockSpec(memory_space=pl.ANY)
    buffers = [pltpu.VMEM((shape[0], block.shape[1]), jnp.float32) for block in blocks] if apart else []
    return pl.pallas_call(
        functools.partial(place_kernel, dims, apart, [[flag for _, flag in terms] for terms, _ in pieces], columns, aliased),
        out_shape=jax.ShapeDtypeStruct(shape, jnp.float32),
        in_specs=[far if apart else near] * len(blocks) + [far] * aliased,
        out_specs=far,
        scratch_shapes=buffers
        + [pltpu.VMEM((shape[0], terms[0][0].shape[1]), jnp.float32) for terms, _ in pieces]
        + [pltpu.SemaphoreType.DMA((len(buffers) + sum(map(len, columns)),))],
        input_output_aliases={len(blocks): 0} if aliased else {},
        compiler_params=pltpu.CompilerParams(vmem_limit_bytes=VMEM_LIMIT),
        cost_estimate=FREE,
        name=name,
    )(*blocks, *([into] if aliased else []))


def ringed(log_derivs, coefficients):
    rows, params = log_derivs.shape
    samples = rows * lax.axis_size("smp")
    levels, planes = lax.axis_size("smp") // 4, lax.axis_size("par")
    per_plane = levels // planes
    shape = (rows, rows * 4 * per_plane)
    scale = 1.0 / samples

    def moves(to):
        pairs = []
        for z in range(levels):
            for x in range(2):
                for c in range(2):
                    for y in range(planes):
                        tz, tx, tc, ty = to(z, x, c, y)
                        target = ((tz % levels) * 2 + tx) * 2 + tc
                        pairs.append((((z * 2 + x) * 2 + c) * planes + y, target * planes + ty))
        return pairs

    def holder(z):
        return z % levels // per_plane

    ring = moves(lambda z, x, c, y: (z + 1 - 2 * c, x, c, y))
    back = moves(lambda z, x, c, y: (z - 1 + 2 * c, x, c, y))
    over_core = moves(lambda z, x, c, y: (z, x, 1 - c, y))
    over_side = moves(lambda z, x, c, y: (z, 1 - x, c, y))
    over_plane = moves(lambda z, x, c, y: (z, x, c, 1 - y))
    diagonal = moves(lambda z, x, c, y: (z, 1 - x, c, 1 - y))
    turns = [moves(lambda z, x, c, y, k=k: (z + k, x, c, y)) for k in range(1, levels)]

    def to_holder(step, side, swap):
        def to(z, x, c, y):
            plane = holder(z - step * (1 - 2 * c))
            return z, x ^ side, c ^ swap ^ (plane != y), plane

        return [(source, target) for source, target in moves(to) if source != target]

    def send(value, pairs):
        return lax.ppermute(value, BOTH, pairs)

    dims = levels, planes, rows // 128

    core_rows = send(log_derivs, over_core)
    one = send(log_derivs, ring)


    coefficients = coefficients[None, :]
    other_coefficients = send(coefficients, over_core)
    side_rows = send(after(log_derivs, other_coefficients), over_side)
    stats = block_stats(log_derivs, core_rows, coefficients, other_coefficients)
    stats = merge(stats, *[send(stats, turn) for turn in turns])
    one, side_rows = lax.optimization_barrier((one, side_rows, stats))[:2]
    two = send(one, ring)
    stats = merge(stats, send(stats, over_side))
    side_core_rows = send(side_rows, over_core)
    all_rows = (log_derivs, core_rows, side_rows, side_core_rows)

    def one_level(block, step, name):
        out = kernel_call(
            functools.partial(one_level_kernel, scale, dims, 9 if step == 1 else 10),
            [(rows, rows)] * 4,
            name,
            stats,
            *all_rows,
            block,
            )
        sent = [[send(out[2 * k + swap], to_holder(step, 1 - k, swap)) for swap in range(2)] for k in range(2)]
        return out, ([*sent[1], (out[2], 9 if step == 1 else 10)], sent[0])

    out, near = one_level(one, 1, "products_near")
    share = params // lax.axis_size("smp")

    own_level = kernel_call(
        functools.partial(own_level_kernel, scale),
        [(2 * rows, rows)] * 2,
        "products_level",
        stats,
        *all_rows,
        after(log_derivs, out[0]),
    )
    near = [*[after(piece, *near[1]) for piece in near[0][:2]], near[0][2]], near[1]
    three = send(after(log_derivs, *near[1], *near[0][:2], *own_level), back)
    two = after(two, *near[1], *near[0][:2], *own_level)
    keep_own, keep_side, sent_own, sent_side = kernel_call(
        functools.partial(across_level_kernel, scale, dims),
        [(2 * rows, rows)] * 4,
        "products_across",
        stats,
        *all_rows,
        two,
        *own_level,
        cost=LONG,
    )
    got_own = send(sent_own, over_plane)
    got_side = send(sent_side, diagonal)
    from_side = send(keep_side, over_side)

    gram = place(dims, [(near[0], [(1, 0)]), (near[1], [(2, 0)])], shape, None, "place_near", apart=True)
    three = after(three, gram)

    out, far = one_level(three, -1, "products_far")

    got_own = after(got_own, out[0])
    own, side = kernel_call(across_kernel, [(rows, rows)] * 2, "sum_across", keep_own, got_own, from_side, got_side)
    across_own, across_side = send(own, over_core), send(side, over_core)
    update = lax.dynamic_slice(after(stats, out[0]), (1, lax.axis_index("smp") * share), (1, share))[0]
    update = update / jnp.sqrt(jnp.float32(samples))
    gram = place(
        dims,
        [((keep_own, got_own), [(5, 0)]), ((from_side, got_side), [(6, 0)])],
        shape,
        gram,
        "place_most",
        apart=True,
    )
    gram = after(gram, *far[1], *far[0][:2])
    gram = place(
        dims,
        [(far[1], [(4, 0)]), (far[0], [(3, 0)]), ((across_own,), [(7, 0)]), ((across_side,), [(8, 0)])],
        shape,
        gram,
        "place_last",
    )
    return (gram, update)


def solution(mesh):
    placed = (P("smp", "par"), P("smp"))
    levels, planes = mesh.shape["smp"] // 4, mesh.shape["par"]
    return jax.shard_map(
        ringed if planes == 2 and levels == 2 * planes else gathered,
        mesh=mesh,
        in_specs=placed,
        out_specs=(P("smp", "par"), P(("par", "smp"))),
        check_vma=False,
    )
```

```python
import functools

import jax
import jax.numpy as jnp
from jax import lax
from jax.experimental import pallas as pl
from jax.experimental.pallas import tpu as pltpu
from jax.sharding import PartitionSpec as P

BOTH = ("smp", "par")
VMEM_LIMIT = 16 * 1024 * 1024
LONG = pl.CostEstimate(flops=4_000_000_000, bytes_accessed=0, transcendentals=0)
FREE = pl.CostEstimate(flops=0, bytes_accessed=0, transcendentals=0)


def row_products(left_rows, right_rows):
    return lax.dot_general(
        left_rows,
        right_rows,
        (((1,), (1,)), ((), ())),
        precision=lax.Precision.HIGHEST,
        preferred_element_type=jnp.float32,
    )


def gathered(log_derivs, coefficients):
    samples = log_derivs.shape[0] * lax.axis_size("smp")
    column_total = lax.psum(jnp.sum(log_derivs, axis=0), "smp")
    centred = (log_derivs - column_total[None, :] / samples) / jnp.sqrt(jnp.float32(samples))
    partial_gram = row_products(centred, lax.all_gather(centred, "smp", axis=0, tiled=True))
    gram = lax.psum_scatter(partial_gram, "par", scatter_dimension=1, tiled=True)
    update_term = lax.dot_general(
        coefficients,
        centred,
        (((0,), (0,)), ((), ())),
        precision=lax.Precision.HIGHEST,
        preferred_element_type=jnp.float32,
    )
    update = lax.psum_scatter(update_term, "smp", scatter_dimension=0, tiled=True)
    return (gram, update)


def after(value, *others):
    return lax.optimization_barrier((value, *others))[0]


def stats_kernel(rows_ref, other_ref, coef_ref, other_coef_ref, stats_ref):
    blocks = (rows_ref, other_ref)
    mean = sum(jnp.sum(ref[...], axis=0, keepdims=True) for ref in blocks) / sum(ref.shape[0] for ref in blocks)
    stats_ref[...] = jnp.zeros_like(stats_ref)
    stats_ref[0:1, :] = mean
    stats_ref[1:2, :] = sum(
        jnp.dot(coef[...], ref[...] - mean, precision=lax.Precision.HIGHEST, preferred_element_type=jnp.float32)
        for coef, ref in zip((coef_ref, other_coef_ref), blocks)
    )
    total = sum(jnp.sum(coef[...], axis=1, keepdims=True) for coef in (coef_ref, other_coef_ref))
    stats_ref[2:3, :] = jnp.broadcast_to(total, mean.shape)


def block_stats(rows, other, coefficients, other_coefficients):
    return kernel_call(
        stats_kernel, [(8, rows.shape[1])], "block_stats", rows, other, coefficients, other_coefficients
    )[0]


def merge_kernel(count, *refs):
    parts, out = refs[:count], refs[count]
    mean = sum(p[0:1, :] for p in parts) / count
    out[...] = jnp.zeros_like(out)
    out[0:1, :] = mean
    out[1:2, :] = sum(p[1:2, :] + p[2:3, :] * (p[0:1, :] - mean) for p in parts)
    out[2:3, :] = sum(p[2:3, :] for p in parts)


def merge(*parts):
    return kernel_call(functools.partial(merge_kernel, len(parts)), [parts[0].shape], "merge", *parts)[0]


def split(values):
    high = values.astype(jnp.bfloat16)
    return high, (values - high.astype(jnp.float32)).astype(jnp.bfloat16)


def dot_nt(left, right):
    return lax.dot_general(left, right, (((1,), (1,)), ((), ())), preferred_element_type=jnp.float32)


def entry(dims, which):
    levels, planes, block = dims
    per_plane = levels // planes
    here, plane = lax.axis_index("smp"), lax.axis_index("par")
    level, side, core = lax.div(here, 4), lax.rem(lax.div(here, 2), 2), lax.rem(here, 2)

    def off(step, core):
        return lax.rem(level - step * (1 - 2 * core) + levels, levels)

    def held(z):
        return lax.div(z, per_plane) == plane

    if which == 0:
        return held(level)
    if which >= 9:
        return held(off(1 if which == 9 else -1, core))
    if which <= 4:
        step = 1 if which <= 2 else -1
        first = held(off(step, 0))
        z, of_core = jnp.where(first, off(step, 0), off(step, 1)), jnp.where(first, 0, 1)
    else:
        z = jnp.where(held(level), level, lax.rem(level + levels // 2, levels))
        of_core = core if which <= 6 else 1 - core
    of_side = side if which % 2 == 1 else 1 - side
    return ((lax.rem(z, per_plane) * 2 + of_side) * 2 + of_core) * block


def product_of(row_ref, mean, high, low, scale):
    row_high, row_low = split(row_ref[...] - mean)
    return (dot_nt(row_high, high) + (dot_nt(row_high, low) + dot_nt(row_low, high))) * scale


def one_level_kernel(scale, dims, flag_at, mean_ref, *refs):
    rows, block, outs = refs[:4], refs[4], refs[5:]
    mean = mean_ref[0:1, :]
    high, low = split(block[...] - mean)
    straight = entry(dims, flag_at)
    for k, side in enumerate((1, 0)):
        same = product_of(rows[2 * side], mean, high, low, scale)
        other = product_of(rows[2 * side + 1], mean, high, low, scale)
        outs[2 * k][...] = jnp.where(straight, same, other)
        outs[2 * k + 1][...] = jnp.where(straight, other, same)


def own_level_kernel(scale, mean_ref, *refs):
    rows, block, outs = refs[:4], refs[4], refs[5:]
    mean = mean_ref[0:1, :]
    high, low = split(block[...] - mean)
    height = rows[0].shape[0]
    for k, row in enumerate(rows):
        outs[k // 2][k % 2 * height : (k % 2 + 1) * height, :] = product_of(row, mean, high, low, scale)


def across_level_kernel(scale, dims, mean_ref, *refs):
    rows, block, level, outs = refs[:4], refs[4], refs[5:7], refs[7:]
    mean = mean_ref[0:1, :]
    first = entry(dims, 0)
    high, low = split(block[...] - mean)
    height = rows[0].shape[0]
    for k, row in enumerate(rows):
        total = product_of(row, mean, high, low, scale)
        place = slice(k % 2 * height, (k % 2 + 1) * height)
        here = level[k // 2][place, :]
        outs[k // 2][place, :] = jnp.where(first, here, total)
        outs[2 + k // 2][place, :] = jnp.where(first, total, here)


def across_kernel(keep_own, got_own, from_side, got_side, own, side):
    height = own.shape[0]
    own[...] = keep_own[height:, :] + got_own[height:, :]
    side[...] = from_side[height:, :] + got_side[height:, :]


def kernel_call(kernel, out_shapes, name, *args, cost=FREE):
    return pl.pallas_call(
        kernel,
        out_shape=[jax.ShapeDtypeStruct(s, jnp.float32) for s in out_shapes],
        in_specs=[pl.BlockSpec(memory_space=pltpu.VMEM)] * len(args),
        out_specs=[pl.BlockSpec(memory_space=pltpu.VMEM)] * len(out_shapes),
        compiler_params=pltpu.CompilerParams(vmem_limit_bytes=VMEM_LIMIT),
        cost_estimate=cost,
        name=name,
    )(*args)


def place_kernel(dims, apart, summands, columns, aliased, *refs):
    blocks = list(refs[: sum(map(len, summands))])
    out = refs[len(blocks) + aliased]
    scratch = list(refs[len(blocks) + aliased + 1 :])
    sems = scratch.pop()
    if apart:
        loads = []
        for block in blocks:
            here = scratch.pop(0)
            loads.append(pltpu.make_async_copy(block.at[pl.ds(0, here.shape[0])], here, sems.at[len(loads)]))
            loads[-1].start()
        blocks = [load.dst_ref for load in loads]
        for load in loads:
            load.wait()
    copies = []
    for total, flags, places in zip(scratch, summands, columns):
        taken, blocks = blocks[: len(flags)], blocks[len(flags) :]
        value = 0.0
        for block, flag_at in zip(taken, flags):
            part = block[0 : total.shape[0], :]
            value += part if flag_at is None else jnp.where(entry(dims, flag_at), part, 0.0)
        total[...] = value
        width = total.shape[1] // len(places)
        for part, (where, offset) in enumerate(places):
            column = pl.multiple_of((entry(dims, where) + offset) * 128, 128)
            copy = pltpu.make_async_copy(
                total.at[:, pl.ds(part * width, width)],
                out.at[:, pl.ds(column, width)],
                sems.at[apart * sum(map(len, summands)) + len(copies)],
            )
            copy.start()
            copies.append(copy)
    for copy in copies:
        copy.wait()


def place(dims, pieces, shape, into, name, apart=False):
    pieces = [([t if isinstance(t, tuple) else (t, None) for t in terms], places) for terms, places in pieces]
    blocks = [block for terms, _ in pieces for block, _ in terms]
    columns = [places for _, places in pieces]
    aliased = 0 if into is None else 1
    near, far = pl.BlockSpec(memory_space=pltpu.VMEM), pl.BlockSpec(memory_space=pl.ANY)
    buffers = [pltpu.VMEM((shape[0], block.shape[1]), jnp.float32) for block in blocks] if apart else []
    return pl.pallas_call(
        functools.partial(place_kernel, dims, apart, [[flag for _, flag in terms] for terms, _ in pieces], columns, aliased),
        out_shape=jax.ShapeDtypeStruct(shape, jnp.float32),
        in_specs=[far if apart else near] * len(blocks) + [far] * aliased,
        out_specs=far,
        scratch_shapes=buffers
        + [pltpu.VMEM((shape[0], terms[0][0].shape[1]), jnp.float32) for terms, _ in pieces]
        + [pltpu.SemaphoreType.DMA((len(buffers) + sum(map(len, columns)),))],
        input_output_aliases={len(blocks): 0} if aliased else {},
        compiler_params=pltpu.CompilerParams(vmem_limit_bytes=VMEM_LIMIT),
        cost_estimate=FREE,
        name=name,
    )(*blocks, *([into] if aliased else []))


def ringed(log_derivs, coefficients):
    rows, params = log_derivs.shape
    samples = rows * lax.axis_size("smp")
    levels, planes = lax.axis_size("smp") // 4, lax.axis_size("par")
    per_plane = levels // planes
    shape = (rows, rows * 4 * per_plane)
    scale = 1.0 / samples

    def moves(to):
        pairs = []
        for z in range(levels):
            for x in range(2):
                for c in range(2):
                    for y in range(planes):
                        tz, tx, tc, ty = to(z, x, c, y)
                        target = ((tz % levels) * 2 + tx) * 2 + tc
                        pairs.append((((z * 2 + x) * 2 + c) * planes + y, target * planes + ty))
        return pairs

    def holder(z):
        return z % levels // per_plane

    ring = moves(lambda z, x, c, y: (z + 1 - 2 * c, x, c, y))
    back = moves(lambda z, x, c, y: (z - 1 + 2 * c, x, c, y))
    over_core = moves(lambda z, x, c, y: (z, x, 1 - c, y))
    over_side = moves(lambda z, x, c, y: (z, 1 - x, c, y))
    over_plane = moves(lambda z, x, c, y: (z, x, c, 1 - y))
    diagonal = moves(lambda z, x, c, y: (z, 1 - x, c, 1 - y))
    turns = [moves(lambda z, x, c, y, k=k: (z + k, x, c, y)) for k in range(1, levels)]

    def to_holder(step, side, swap):
        def to(z, x, c, y):
            plane = holder(z - step * (1 - 2 * c))
            return z, x ^ side, c ^ swap ^ (plane != y), plane

        return [(source, target) for source, target in moves(to) if source != target]

    def send(value, pairs):
        return lax.ppermute(value, BOTH, pairs)

    dims = levels, planes, rows // 128

    one = send(log_derivs, ring)


    coefficients = coefficients[None, :]
    other_coefficients = send(coefficients, over_core)
    core_rows = send(after(log_derivs, other_coefficients), over_core)
    side_rows = send(after(log_derivs, other_coefficients), over_side)
    stats = block_stats(log_derivs, core_rows, coefficients, other_coefficients)
    stats = merge(stats, *[send(stats, turn) for turn in turns])
    one, side_rows = lax.optimization_barrier((one, side_rows, stats))[:2]
    two = send(one, ring)
    stats = merge(stats, send(stats, over_side))
    side_core_rows = send(side_rows, over_core)
    all_rows = (log_derivs, core_rows, side_rows, side_core_rows)

    def one_level(block, step, name):
        out = kernel_call(
            functools.partial(one_level_kernel, scale, dims, 9 if step == 1 else 10),
            [(rows, rows)] * 4,
            name,
            stats,
            *all_rows,
            block,
            )
        sent = [[send(out[2 * k + swap], to_holder(step, 1 - k, swap)) for swap in range(2)] for k in range(2)]
        return out, ([*sent[1], (out[2], 9 if step == 1 else 10)], sent[0])

    out, near = one_level(one, 1, "products_near")
    share = params // lax.axis_size("smp")

    own_level = kernel_call(
        functools.partial(own_level_kernel, scale),
        [(2 * rows, rows)] * 2,
        "products_level",
        stats,
        *all_rows,
        after(log_derivs, out[0]),
    )
    near = [*[after(piece, *near[1]) for piece in near[0][:2]], near[0][2]], near[1]
    three = send(after(log_derivs, *near[1], *near[0][:2], *own_level), back)
    two = after(two, *near[1], *near[0][:2], *own_level)
    keep_own, keep_side, sent_own, sent_side = kernel_call(
        functools.partial(across_level_kernel, scale, dims),
        [(2 * rows, rows)] * 4,
        "products_across",
        stats,
        *all_rows,
        two,
        *own_level,
        cost=LONG,
    )
    got_own = send(sent_own, over_plane)
    got_side = send(sent_side, diagonal)
    from_side = send(keep_side, over_side)

    gram = place(dims, [(near[0], [(1, 0)]), (near[1], [(2, 0)])], shape, None, "place_near", apart=True)
    three = after(three, gram)

    out, far = one_level(three, -1, "products_far")

    got_own = after(got_own, out[0])
    own, side = kernel_call(across_kernel, [(rows, rows)] * 2, "sum_across", keep_own, got_own, from_side, got_side)
    across_own, across_side = send(own, over_core), send(side, over_core)
    update = lax.dynamic_slice(after(stats, out[0]), (1, lax.axis_index("smp") * share), (1, share))[0]
    update = update / jnp.sqrt(jnp.float32(samples))
    gram = place(
        dims,
        [((keep_own, got_own), [(5, 0)]), ((from_side, got_side), [(6, 0)])],
        shape,
        gram,
        "place_most",
        apart=True,
    )
    gram = after(gram, *far[1], *far[0][:2])
    gram = place(
        dims,
        [(far[1], [(4, 0)]), (far[0], [(3, 0)]), ((across_own,), [(7, 0)]), ((across_side,), [(8, 0)])],
        shape,
        gram,
        "place_last",
    )
    return (gram, update)


def solution(mesh):
    placed = (P("smp", "par"), P("smp"))
    levels, planes = mesh.shape["smp"] // 4, mesh.shape["par"]
    return jax.shard_map(
        ringed if planes == 2 and levels == 2 * planes else gathered,
        mesh=mesh,
        in_specs=placed,
        out_specs=(P("smp", "par"), P(("par", "smp"))),
        check_vma=False,
    )
```

```python
import functools

import jax
import jax.numpy as jnp
from jax import lax
from jax.experimental import pallas as pl
from jax.experimental.pallas import tpu as pltpu
from jax.sharding import PartitionSpec as P

BOTH = ("smp", "par")
VMEM_LIMIT = 10 * 1024 * 1024
LONG = pl.CostEstimate(flops=4_000_000_000, bytes_accessed=0, transcendentals=0)
FREE = pl.CostEstimate(flops=0, bytes_accessed=0, transcendentals=0)


def row_products(left_rows, right_rows):
    return lax.dot_general(
        left_rows,
        right_rows,
        (((1,), (1,)), ((), ())),
        precision=lax.Precision.HIGHEST,
        preferred_element_type=jnp.float32,
    )


def gathered(log_derivs, coefficients):
    samples = log_derivs.shape[0] * lax.axis_size("smp")
    column_total = lax.psum(jnp.sum(log_derivs, axis=0), "smp")
    centred = (log_derivs - column_total[None, :] / samples) / jnp.sqrt(jnp.float32(samples))
    partial_gram = row_products(centred, lax.all_gather(centred, "smp", axis=0, tiled=True))
    gram = lax.psum_scatter(partial_gram, "par", scatter_dimension=1, tiled=True)
    update_term = lax.dot_general(
        coefficients,
        centred,
        (((0,), (0,)), ((), ())),
        precision=lax.Precision.HIGHEST,
        preferred_element_type=jnp.float32,
    )
    update = lax.psum_scatter(update_term, "smp", scatter_dimension=0, tiled=True)
    return (gram, update)


def after(value, *others):
    return lax.optimization_barrier((value, *others))[0]


def stats_kernel(rows_ref, other_ref, coef_ref, other_coef_ref, stats_ref):
    blocks = (rows_ref, other_ref)
    mean = sum(jnp.sum(ref[...], axis=0, keepdims=True) for ref in blocks) / sum(ref.shape[0] for ref in blocks)
    stats_ref[...] = jnp.zeros_like(stats_ref)
    stats_ref[0:1, :] = mean
    stats_ref[1:2, :] = sum(
        jnp.dot(coef[...], ref[...] - mean, precision=lax.Precision.HIGHEST, preferred_element_type=jnp.float32)
        for coef, ref in zip((coef_ref, other_coef_ref), blocks)
    )
    total = sum(jnp.sum(coef[...], axis=1, keepdims=True) for coef in (coef_ref, other_coef_ref))
    stats_ref[2:3, :] = jnp.broadcast_to(total, mean.shape)


def block_stats(rows, other, coefficients, other_coefficients):
    return kernel_call(
        stats_kernel, [(8, rows.shape[1])], "block_stats", rows, other, coefficients, other_coefficients
    )[0]


def merge_kernel(count, *refs):
    parts, out = refs[:count], refs[count]
    mean = sum(p[0:1, :] for p in parts) / count
    out[...] = jnp.zeros_like(out)
    out[0:1, :] = mean
    out[1:2, :] = sum(p[1:2, :] + p[2:3, :] * (p[0:1, :] - mean) for p in parts)
    out[2:3, :] = sum(p[2:3, :] for p in parts)


def merge(*parts):
    return kernel_call(functools.partial(merge_kernel, len(parts)), [parts[0].shape], "merge", *parts)[0]


def split(values):
    high = values.astype(jnp.bfloat16)
    return high, (values - high.astype(jnp.float32)).astype(jnp.bfloat16)


def dot_nt(left, right):
    return lax.dot_general(left, right, (((1,), (1,)), ((), ())), preferred_element_type=jnp.float32)


def entry(dims, which):
    levels, planes, block = dims
    per_plane = levels // planes
    here, plane = lax.axis_index("smp"), lax.axis_index("par")
    level, side, core = lax.div(here, 4), lax.rem(lax.div(here, 2), 2), lax.rem(here, 2)

    def off(step, core):
        return lax.rem(level - step * (1 - 2 * core) + levels, levels)

    def held(z):
        return lax.div(z, per_plane) == plane

    if which == 0:
        return held(level)
    if which >= 9:
        return held(off(1 if which == 9 else -1, core))
    if which <= 4:
        step = 1 if which <= 2 else -1
        first = held(off(step, 0))
        z, of_core = jnp.where(first, off(step, 0), off(step, 1)), jnp.where(first, 0, 1)
    else:
        z = jnp.where(held(level), level, lax.rem(level + levels // 2, levels))
        of_core = core if which <= 6 else 1 - core
    of_side = side if which % 2 == 1 else 1 - side
    return ((lax.rem(z, per_plane) * 2 + of_side) * 2 + of_core) * block


def product_of(row_ref, mean, high, low, scale):
    row_high, row_low = split(row_ref[...] - mean)
    return (dot_nt(row_high, high) + (dot_nt(row_high, low) + dot_nt(row_low, high))) * scale


def one_level_kernel(scale, dims, flag_at, mean_ref, *refs):
    rows, block, outs = refs[:4], refs[4], refs[5:]
    mean = mean_ref[0:1, :]
    high, low = split(block[...] - mean)
    straight = entry(dims, flag_at)
    for k, side in enumerate((1, 0)):
        same = product_of(rows[2 * side], mean, high, low, scale)
        other = product_of(rows[2 * side + 1], mean, high, low, scale)
        outs[2 * k][...] = jnp.where(straight, same, other)
        outs[2 * k + 1][...] = jnp.where(straight, other, same)


def own_level_kernel(scale, mean_ref, *refs):
    rows, block, outs = refs[:4], refs[4], refs[5:]
    mean = mean_ref[0:1, :]
    high, low = split(block[...] - mean)
    height = rows[0].shape[0]
    for k, row in enumerate(rows):
        outs[k // 2][k % 2 * height : (k % 2 + 1) * height, :] = product_of(row, mean, high, low, scale)


def across_level_kernel(scale, dims, mean_ref, *refs):
    rows, block, level, outs = refs[:4], refs[4], refs[5:7], refs[7:]
    mean = mean_ref[0:1, :]
    first = entry(dims, 0)
    high, low = split(block[...] - mean)
    height = rows[0].shape[0]
    for k, row in enumerate(rows):
        total = product_of(row, mean, high, low, scale)
        place = slice(k % 2 * height, (k % 2 + 1) * height)
        here = level[k // 2][place, :]
        outs[k // 2][place, :] = jnp.where(first, here, total)
        outs[2 + k // 2][place, :] = jnp.where(first, total, here)


def across_kernel(keep_own, got_own, from_side, got_side, own, side):
    height = own.shape[0]
    own[...] = keep_own[height:, :] + got_own[height:, :]
    side[...] = from_side[height:, :] + got_side[height:, :]


def kernel_call(kernel, out_shapes, name, *args, cost=FREE):
    return pl.pallas_call(
        kernel,
        out_shape=[jax.ShapeDtypeStruct(s, jnp.float32) for s in out_shapes],
        in_specs=[pl.BlockSpec(memory_space=pltpu.VMEM)] * len(args),
        out_specs=[pl.BlockSpec(memory_space=pltpu.VMEM)] * len(out_shapes),
        compiler_params=pltpu.CompilerParams(vmem_limit_bytes=VMEM_LIMIT),
        cost_estimate=cost,
        name=name,
    )(*args)


def place_kernel(dims, apart, summands, columns, aliased, *refs):
    blocks = list(refs[: sum(map(len, summands))])
    out = refs[len(blocks) + aliased]
    scratch = list(refs[len(blocks) + aliased + 1 :])
    sems = scratch.pop()
    if apart:
        loads = []
        for block in blocks:
            here = scratch.pop(0)
            loads.append(pltpu.make_async_copy(block.at[pl.ds(0, here.shape[0])], here, sems.at[len(loads)]))
            loads[-1].start()
        blocks = [load.dst_ref for load in loads]
        for load in loads:
            load.wait()
    copies = []
    for total, flags, places in zip(scratch, summands, columns):
        taken, blocks = blocks[: len(flags)], blocks[len(flags) :]
        value = 0.0
        for block, flag_at in zip(taken, flags):
            part = block[0 : total.shape[0], :]
            value += part if flag_at is None else jnp.where(entry(dims, flag_at), part, 0.0)
        total[...] = value
        width = total.shape[1] // len(places)
        for part, (where, offset) in enumerate(places):
            column = pl.multiple_of((entry(dims, where) + offset) * 128, 128)
            copy = pltpu.make_async_copy(
                total.at[:, pl.ds(part * width, width)],
                out.at[:, pl.ds(column, width)],
                sems.at[apart * sum(map(len, summands)) + len(copies)],
            )
            copy.start()
            copies.append(copy)
    for copy in copies:
        copy.wait()


def place(dims, pieces, shape, into, name, apart=False):
    pieces = [([t if isinstance(t, tuple) else (t, None) for t in terms], places) for terms, places in pieces]
    blocks = [block for terms, _ in pieces for block, _ in terms]
    columns = [places for _, places in pieces]
    aliased = 0 if into is None else 1
    near, far = pl.BlockSpec(memory_space=pltpu.VMEM), pl.BlockSpec(memory_space=pl.ANY)
    buffers = [pltpu.VMEM((shape[0], block.shape[1]), jnp.float32) for block in blocks] if apart else []
    return pl.pallas_call(
        functools.partial(place_kernel, dims, apart, [[flag for _, flag in terms] for terms, _ in pieces], columns, aliased),
        out_shape=jax.ShapeDtypeStruct(shape, jnp.float32),
        in_specs=[far if apart else near] * len(blocks) + [far] * aliased,
        out_specs=far,
        scratch_shapes=buffers
        + [pltpu.VMEM((shape[0], terms[0][0].shape[1]), jnp.float32) for terms, _ in pieces]
        + [pltpu.SemaphoreType.DMA((len(buffers) + sum(map(len, columns)),))],
        input_output_aliases={len(blocks): 0} if aliased else {},
        compiler_params=pltpu.CompilerParams(vmem_limit_bytes=VMEM_LIMIT),
        cost_estimate=FREE,
        name=name,
    )(*blocks, *([into] if aliased else []))


def ringed(log_derivs, coefficients):
    rows, params = log_derivs.shape
    samples = rows * lax.axis_size("smp")
    levels, planes = lax.axis_size("smp") // 4, lax.axis_size("par")
    per_plane = levels // planes
    shape = (rows, rows * 4 * per_plane)
    scale = 1.0 / samples

    def moves(to):
        pairs = []
        for z in range(levels):
            for x in range(2):
                for c in range(2):
                    for y in range(planes):
                        tz, tx, tc, ty = to(z, x, c, y)
                        target = ((tz % levels) * 2 + tx) * 2 + tc
                        pairs.append((((z * 2 + x) * 2 + c) * planes + y, target * planes + ty))
        return pairs

    def holder(z):
        return z % levels // per_plane

    ring = moves(lambda z, x, c, y: (z + 1 - 2 * c, x, c, y))
    back = moves(lambda z, x, c, y: (z - 1 + 2 * c, x, c, y))
    over_core = moves(lambda z, x, c, y: (z, x, 1 - c, y))
    over_side = moves(lambda z, x, c, y: (z, 1 - x, c, y))
    over_plane = moves(lambda z, x, c, y: (z, x, c, 1 - y))
    diagonal = moves(lambda z, x, c, y: (z, 1 - x, c, 1 - y))
    turns = [moves(lambda z, x, c, y, k=k: (z + k, x, c, y)) for k in range(1, levels)]

    def to_holder(step, side, swap):
        def to(z, x, c, y):
            plane = holder(z - step * (1 - 2 * c))
            return z, x ^ side, c ^ swap ^ (plane != y), plane

        return [(source, target) for source, target in moves(to) if source != target]

    def send(value, pairs):
        return lax.ppermute(value, BOTH, pairs)

    dims = levels, planes, rows // 128

    core_rows = send(log_derivs, over_core)
    one = send(log_derivs, ring)


    coefficients = coefficients[None, :]
    other_coefficients = send(coefficients, over_core)
    side_rows = send(after(log_derivs, other_coefficients), over_side)
    stats = block_stats(log_derivs, core_rows, coefficients, other_coefficients)
    stats = merge(stats, *[send(stats, turn) for turn in turns])
    one, side_rows = lax.optimization_barrier((one, side_rows, stats))[:2]
    two = send(one, ring)
    stats = merge(stats, send(stats, over_side))
    side_core_rows = send(side_rows, over_core)
    all_rows = (log_derivs, core_rows, side_rows, side_core_rows)

    def one_level(block, step, name):
        out = kernel_call(
            functools.partial(one_level_kernel, scale, dims, 9 if step == 1 else 10),
            [(rows, rows)] * 4,
            name,
            stats,
            *all_rows,
            block,
            )
        sent = [[send(out[2 * k + swap], to_holder(step, 1 - k, swap)) for swap in range(2)] for k in range(2)]
        return out, ([*sent[1], (out[2], 9 if step == 1 else 10)], sent[0])

    out, near = one_level(one, 1, "products_near")
    share = params // lax.axis_size("smp")

    own_level = kernel_call(
        functools.partial(own_level_kernel, scale),
        [(2 * rows, rows)] * 2,
        "products_level",
        stats,
        *all_rows,
        after(log_derivs, out[0]),
    )
    near = [*[after(piece, *near[1]) for piece in near[0][:2]], near[0][2]], near[1]
    three = send(after(log_derivs, *near[1], *near[0][:2], *own_level), back)
    two = after(two, *near[1], *near[0][:2], *own_level)
    keep_own, keep_side, sent_own, sent_side = kernel_call(
        functools.partial(across_level_kernel, scale, dims),
        [(2 * rows, rows)] * 4,
        "products_across",
        stats,
        *all_rows,
        two,
        *own_level,
        cost=LONG,
    )
    got_own = send(sent_own, over_plane)
    got_side = send(sent_side, diagonal)
    from_side = send(keep_side, over_side)

    gram = place(dims, [(near[0], [(1, 0)]), (near[1], [(2, 0)])], shape, None, "place_near", apart=True)
    three = after(three, gram)

    out, far = one_level(three, -1, "products_far")

    got_own = after(got_own, out[0])
    own, side = kernel_call(across_kernel, [(rows, rows)] * 2, "sum_across", keep_own, got_own, from_side, got_side)
    across_own, across_side = send(own, over_core), send(side, over_core)
    update = lax.dynamic_slice(after(stats, out[0]), (1, lax.axis_index("smp") * share), (1, share))[0]
    update = update / jnp.sqrt(jnp.float32(samples))
    gram = place(
        dims,
        [((keep_own, got_own), [(5, 0)]), ((from_side, got_side), [(6, 0)])],
        shape,
        gram,
        "place_most",
        apart=True,
    )
    gram = after(gram, *far[1], *far[0][:2])
    gram = place(
        dims,
        [(far[1], [(4, 0)]), (far[0], [(3, 0)]), ((across_own,), [(7, 0)]), ((across_side,), [(8, 0)])],
        shape,
        gram,
        "place_last",
    )
    return (gram, update)


def solution(mesh):
    placed = (P("smp", "par"), P("smp"))
    levels, planes = mesh.shape["smp"] // 4, mesh.shape["par"]
    return jax.shard_map(
        ringed if planes == 2 and levels == 2 * planes else gathered,
        mesh=mesh,
        in_specs=placed,
        out_specs=(P("smp", "par"), P(("par", "smp"))),
        check_vma=False,
    )
```
